256 devices in a mesh: sx: 4 (over x_lo, core), sy: 2 (over x_hi), fsdp: 32 (over z, y).
Axes of the slice: x: 4 (x_hi: 2, x_lo: 2; x = x_hi * 2 + x_lo), y: 4, z: 8, core: 2. Of those that a mesh axis runs over, the one named last changes fastest.
Arguments:
- x_code: bfloat16 [32, 32, 32, 1536], P('fsdp', 'sx', 'sy'), may hold values from -6 to 6
- x_exp: int32 [32, 32, 32, 12], P('fsdp', 'sx', 'sy'), may hold values from -2 to 2
- dw_kernel: float32 [7, 7, 1536], replicated, may hold values from -1.2 to 1.2
- dw_bias: float32 [1536], replicated, may hold values from -4 to 4
- ln_gain: float32 [1536], replicated, may hold values from 0.1 to 1.9
- ln_bias: float32 [1536], replicated, may hold values from -3 to 3
- w_up: bfloat16 [1536, 3072], P('fsdp'), may hold values from -0.15625 to 0.15625
- b_up: float32 [3072], replicated, may hold values from -3 to 3
- w_down: bfloat16 [3072, 1536], P(None, 'fsdp'), may hold values from -0.109375 to 0.109375
- b_down: float32 [1536], replicated, may hold values from -3 to 3
- layer_scale: float32 [1536], replicated, may hold values from 0.3 to 1.5
- cotangent: bfloat16 [32, 32, 32, 1536], P('fsdp', 'sx', 'sy'), may hold values from -6 to 6
Outputs:
- block_out: bfloat16 [32, 32, 32, 1536], P('fsdp', 'sx', 'sy')
- grad_input: bfloat16 [32, 32, 32, 1536], P('fsdp', 'sx', 'sy')
- grad_kernel: float32 [7, 7, 1536], replicated
- grad_gain: float32 [1536], replicated
- grad_scale: float32 [1536], replicated
The draws below stay inside these ranges and needn't reach their ends.
All inputs are finite; a program needn't handle non-finite values.
Results may differ from the reference program's by a relative error of at most 0.006.
Values may be sent and summed in bfloat16 or wider, within the bound.
A program may use at most 192 MiB of HBM per device.

```python
import math
import jax
import jax.numpy as jnp
from jax import lax

C = 1536
FF = 3072
CG = 128
KW = 7
SLIDES = 32
H = 32
W = 32


def with_ends(entries, own_key, low, high):
    index_at = [jax.random.randint(jax.random.fold_in(own_key, axis), (), 0, length) for axis, length in enumerate(entries.shape)]
    main_axis = entries.shape.index(max(entries.shape))
    beside = index_at[:main_axis] + [(index_at[main_axis] + 1) % entries.shape[main_axis]] + index_at[main_axis + 1:]
    return entries.at[tuple(index_at)].set(low).at[tuple(beside)].set(high)


def steps_of(rng, extent, shards, low, high):
    gain, own = 1.0, jax.random.fold_in(rng, 6)
    for position, blocks in shards:
        heights = jnp.exp(jax.random.uniform(jax.random.fold_in(own, position), (blocks,), jnp.float32, low / len(shards), high / len(shards)))
        gain = gain * jnp.repeat(heights, extent[position] // blocks).reshape([-1 if axis == position else 1 for axis in range(len(extent))])
    return gain


def bell_draw(rng, dims, width, bound, pieces=(), kind=jnp.bfloat16):
    values = width * jax.random.normal(rng, dims, jnp.float32)
    if pieces:
        values = values * steps_of(rng, dims, pieces, -0.22, 0.18)
    return jnp.clip(values, -bound, bound).astype(kind)


def setup_inputs(seed: int = 0) -> dict:
    key_list = jax.random.split(jax.random.key(seed), 13)
    x_code = bell_draw(key_list[0], (SLIDES, H, W, C), 1.0, 6.0, ((0, 32), (1, 4), (2, 2)))
    x_exp = with_ends(jax.random.randint(key_list[1], (SLIDES, H, W, C // CG), -2, 3), jax.random.fold_in(key_list[1], 1), -2, 2).astype(jnp.int32)
    dw_kernel = bell_draw(key_list[2], (KW, KW, C), 0.2, 1.2, (), jnp.float32)
    dw_bias = bell_draw(key_list[3], (C,), 0.7, 4.0, (), jnp.float32)
    ln_gain = jnp.clip(1.0 + 0.18 * jax.random.normal(key_list[4], (C,), jnp.float32), 0.1, 1.9)
    ln_bias = bell_draw(key_list[5], (C,), 0.5, 3.0, (), jnp.float32)
    w_up = bell_draw(key_list[6], (C, FF), C ** -0.5, 0.15625, ((0, 32),))
    b_up = bell_draw(key_list[7], (FF,), 0.5, 3.0, (), jnp.float32)
    w_down = bell_draw(key_list[8], (FF, C), FF ** -0.5, 0.109375, ((1, 32),))
    b_down = bell_draw(key_list[9], (C,), 0.5, 3.0, (), jnp.float32)
    layer_scale = jnp.clip(jnp.exp(jax.random.uniform(key_list[10], (C,), jnp.float32, math.log(0.3), math.log(1.5))), 0.3, 1.5)
    cotangent = bell_draw(key_list[11], (SLIDES, H, W, C), 1.0, 6.0, ((0, 32), (1, 4), (2, 2)))
    return dict(x_code=x_code, x_exp=x_exp, dw_kernel=dw_kernel, dw_bias=dw_bias, ln_gain=ln_gain, ln_bias=ln_bias, w_up=w_up, b_up=b_up, w_down=w_down, b_down=b_down, layer_scale=layer_scale, cotangent=cotangent)


def gelu_tanh(v):
    return jax.nn.gelu(v, approximate=True)

def dequantize(code, expo):
    rows, cols, chans = code.shape
    factor = jnp.exp2(expo.astype(jnp.float32))
    grouped = code.astype(jnp.float32).reshape(rows, cols, chans // CG, CG) * factor[..., None]
    return grouped.reshape(rows, cols, chans).astype(jnp.bfloat16)

def one_slide(code, expo, grad_out, dw_kernel, dw_bias, ln_gain, ln_bias, w_up, b_up, w_down, b_down, layer_scale):
    rows, cols, chans = code.shape
    scaled = dequantize(code, expo)
    padded = jnp.pad(scaled.astype(jnp.float32), ((3, 3), (3, 3), (0, 0)))
    conv = jnp.zeros((rows, cols, chans), jnp.float32) + dw_bias
    for i in range(KW):
        for j in range(KW):
            conv = conv + dw_kernel[i, j] * padded[i:i + rows, j:j + cols]
    mean_val = lax.optimization_barrier(jnp.mean(conv, axis=-1, keepdims=True))
    centred = conv - mean_val
    rstd = lax.rsqrt(lax.optimization_barrier(jnp.mean(centred * centred, axis=-1, keepdims=True)) + 1e-06)
    normed = centred * rstd
    ln_out = (normed * ln_gain + ln_bias).astype(jnp.bfloat16).reshape(rows * cols, chans)
    pre = jnp.dot(ln_out, w_up, preferred_element_type=jnp.float32) + b_up
    act, gelu_back = jax.vjp(gelu_tanh, pre)
    mlp = jnp.dot(act.astype(jnp.bfloat16), w_down, preferred_element_type=jnp.float32) + b_down
    mlp = mlp.reshape(rows, cols, chans)
    block_out = (scaled.astype(jnp.float32) + layer_scale * mlp).astype(jnp.bfloat16)
    grad_f = grad_out.astype(jnp.float32)
    scale_term = lax.optimization_barrier(jnp.sum(grad_f * mlp, axis=(0, 1)))
    d_mlp = (layer_scale * grad_f).astype(jnp.bfloat16).reshape(rows * cols, chans)
    d_act = jnp.dot(d_mlp, w_down.T, preferred_element_type=jnp.float32)
    d_pre = gelu_back(d_act)[0].astype(jnp.bfloat16)
    d_ln = jnp.dot(d_pre, w_up.T, preferred_element_type=jnp.float32).reshape(rows, cols, chans)
    gain_term = lax.optimization_barrier(jnp.sum(d_ln * normed, axis=(0, 1)))
    d_norm = d_ln * ln_gain
    d_conv = rstd * (d_norm - lax.optimization_barrier(jnp.mean(d_norm, axis=-1, keepdims=True)) - normed * lax.optimization_barrier(jnp.mean(d_norm * normed, axis=-1, keepdims=True)))
    kernel_rows = []
    for i in range(KW):
        kernel_cols = []
        for j in range(KW):
            kernel_cols.append(lax.optimization_barrier(jnp.sum(d_conv * padded[i:i + rows, j:j + cols], axis=(0, 1))))
        kernel_rows.append(jnp.stack(kernel_cols))
    kernel_term = jnp.stack(kernel_rows)
    padded_grad = jnp.pad(d_conv, ((3, 3), (3, 3), (0, 0)))
    back_conv = grad_f
    for i in range(KW):
        for j in range(KW):
            back_conv = back_conv + dw_kernel[i, j] * padded_grad[6 - i:6 - i + rows, 6 - j:6 - j + cols]
    return (block_out, back_conv.astype(jnp.bfloat16), kernel_term, gain_term, scale_term)

def reference(x_code, x_exp, dw_kernel, dw_bias, ln_gain, ln_bias, w_up, b_up, w_down, b_down, layer_scale, cotangent):

    def per_slide(items):
        return one_slide(items[0], items[1], items[2], dw_kernel, dw_bias, ln_gain, ln_bias, w_up, b_up, w_down, b_down, layer_scale)
    block_out, grad_input, kernel_terms, gain_terms, scale_terms = lax.map(per_slide, (x_code, x_exp, cotangent))
    return (block_out, grad_input, lax.optimization_barrier(jnp.sum(kernel_terms, axis=0)), lax.optimization_barrier(jnp.sum(gain_terms, axis=0)), lax.optimization_barrier(jnp.sum(scale_terms, axis=0)))
```

```python
import functools

import jax
import jax.numpy as jnp
from jax import lax
from jax.experimental import pallas as pl
from jax.experimental.pallas import tpu as pltpu
from jax.sharding import PartitionSpec as P

CG = 128
KW = 7
NB = 12
ROWS, COLS, CHANS = 8, 16, 1536
PR, PC = 16, 32
PIECE = 11
MESH = pl.DeviceIdType.MESH


def remote(src, dst, send, recv, where):
    return pltpu.make_async_remote_copy(
        src_ref=src, dst_ref=dst, send_sem=send, recv_sem=recv, device_id=where, device_id_type=MESH
    )


def row_halo(buf, send, recv, sx, act):
    down = remote(buf.at[:, 8:11, 8:24, :], buf.at[:, 0:3, 8:24, :], send.at[0], recv.at[0], {"sx": sx + 1})
    up = remote(buf.at[:, 3:6, 8:24, :], buf.at[:, 11:14, 8:24, :], send.at[1], recv.at[1], {"sx": sx - 1})
    if act == "start":

        @pl.when(sx < 3)
        def _():
            down.start()

        @pl.when(sx > 0)
        def _():
            up.start()

    else:

        @pl.when(sx < 3)
        def _():
            up.wait_recv()
            down.wait_send()

        @pl.when(sx > 0)
        def _():
            down.wait_recv()
            up.wait_send()


def zero_rows(buf, sx):
    @pl.when(sx == 0)
    def _():
        buf[:, 0:3, :, :] = jnp.zeros((NB, 3, PC, 128), jnp.float32)

    @pl.when(sx == 3)
    def _():
        buf[:, 11:14, :, :] = jnp.zeros((NB, 3, PC, 128), jnp.float32)


def pack_cols(buf, stage, sy):
    for side, first in ((0, 21), (1, 8)):

        @pl.when(sy == side)
        def _():
            @pl.loop(0, NB)
            def _(b):
                for c in range(3):
                    at = pl.multiple_of(b * 16, 16)
                    stage[c, pl.ds(at, 16), :] = buf[b, :, first + c, :].astype(jnp.bfloat16)


def unpack_cols(buf, stage, sy):
    for side, first, other in ((0, 24, 5), (1, 5, 24)):

        @pl.when(sy == side)
        def _():
            @pl.loop(0, NB)
            def _(b):
                for c in range(3):
                    at = pl.multiple_of(b * 16, 16)
                    buf[b, :, first + c, :] = stage[c, pl.ds(at, 16), :].astype(jnp.float32)
                    buf[b, :, other + c, :] = jnp.zeros((PR, 128), jnp.float32)


def lanes(b):
    return pl.ds(pl.multiple_of(b * 128, 128), 128)


def depthwise(buf, b, taps, start, flip):
    acc = start
    for j in range(KW):
        jj = 6 - j if flip else j
        shifted = buf[b, 0:14, 5 + jj : 21 + jj, :]
        for i in range(KW):
            ii = 6 - i if flip else i
            acc = acc + taps[i, j, lanes(b)].reshape(1, 1, 128) * shifted[ii : ii + ROWS]
    return acc


def kernel_grad(xbuf, gbuf, grads, b):
    g = gbuf[b, 3:11, 8:24, :]
    for j in range(KW):
        shifted = xbuf[b, 0:14, 5 + j : 21 + j, :]
        for i in range(KW):
            q = jnp.sum(g * shifted[i : i + ROWS], axis=0)
            grads[b * 7 + i, j, :] = jnp.sum(q, axis=0)


def tail_kernel(
    xp, dc, cot, taps, extra, gi, gk, gg, gs,
    gp, stage, landed, grads, got1, part, got2, fin, full,
    hs, hr, cs, cr, s1, r1, s2, r2, s3, r3, s4, r4,
):
    sx, sy, f = lax.axis_index("sx"), lax.axis_index("sy"), lax.axis_index("fsdp")
    g = sx * 2 + sy

    def peer(k):
        p = lax.rem(g + k, 8)
        return p, {"sx": p // 2, "sy": lax.rem(p, 2)}

    barrier = pltpu.get_barrier_semaphore()
    for k in range(1, 8):
        pl.semaphore_signal(barrier, inc=1, device_id=peer(k)[1], device_id_type=MESH)

    @pl.loop(1, 32)
    def _(k):
        pl.semaphore_signal(barrier, inc=1, device_id={"fsdp": lax.rem(f + k, 32)}, device_id_type=MESH)

    gp[:, 3:11, 8:24, :] = dc[...]
    zero_rows(gp, sx)
    grads[84:88] = jnp.zeros((4, 8, 128), jnp.float32)
    pl.semaphore_wait(barrier, 38)

    row_halo(gp, hs, hr, sx, "start")

    @pl.loop(0, 6)
    def _(b):
        kernel_grad(xp, gp, grads, b)

    row_halo(gp, hs, hr, sx, "wait")
    pack_cols(gp, stage, sy)
    col = remote(stage, landed, cs, cr, {"sy": 1 - sy})
    col.start()

    @pl.loop(6, NB)
    def _(b):
        kernel_grad(xp, gp, grads, b)

    for b in range(NB):
        grads[b * 7, 7, :] = extra[0, b * 128 : (b + 1) * 128]
        grads[b * 7 + 1, 7, :] = extra[1, b * 128 : (b + 1) * 128]
        for i in range(2, 7):
            grads[b * 7 + i, 7, :] = jnp.zeros((128,), jnp.float32)

    first = []
    for k in range(1, 8):
        p, where = peer(k)
        first.append(remote(grads.at[pl.ds(p * PIECE, PIECE)], got1.at[k - 1], s1.at[k - 1], r1.at[k - 1], where))
        first[-1].start()

    col.wait()
    unpack_cols(gp, landed, sy)

    def out_conv(b):
        gi[:, :, lanes(b)] = depthwise(
            gp, b, taps, cot[:, :, lanes(b)].astype(jnp.float32), True
        ).astype(jnp.bfloat16)

    pl.loop(0, 4)(out_conv)

    total = grads[pl.ds(g * PIECE, PIECE)]
    for k in range(7):
        first[k].wait_recv()
        total = total + got1[k]
    part[...] = total

    def to_owner(t):
        owner = t * 3
        slot = lax.rem(f - owner + 32, 32)
        return remote(part.at[t], got2.at[slot], s2.at[t], r2.at[slot], {"fsdp": owner})

    for t in range(PIECE):

        @pl.when(f != t * 3)
        def _():
            to_owner(t).start()

    pl.loop(4, 8)(out_conv)

    mine = f // 3
    owns = lax.rem(f, 3) == 0

    def spread(k):
        return remote(fin.at[mine], fin.at[mine], s3.at[k], r3.at[mine], {"fsdp": lax.rem(f + k, 32)})

    @pl.when(owns)
    def _():
        fin[mine] = part[mine]

        @pl.loop(1, 32)
        def _(k):
            remote(part.at[0], got2.at[k], s2.at[0], r2.at[k], {"fsdp": f}).wait_recv()
            fin[mine] = fin[mine] + got2[k]

        @pl.loop(1, 32)
        def _(k):
            spread(k).start()

    pl.loop(8, NB)(out_conv)

    for t in range(PIECE):

        @pl.when(f != t * 3)
        def _():
            remote(fin.at[t], fin.at[t], s3.at[0], r3.at[t], {"fsdp": t * 3}).wait_recv()

    last = []
    for k in range(1, 8):
        p, where = peer(k)
        last.append(remote(fin, full.at[pl.ds(g * PIECE, PIECE)], s4.at[k - 1], r4.at[k - 1], where))
        last[-1].start()
    full[pl.ds(g * PIECE, PIECE)] = fin[...]
    for k in range(7):
        last[k].wait_recv()
    for b in range(NB):
        at = slice(b * 128, (b + 1) * 128)
        for i in range(KW):
            gk[i, :, at] = full[b * 7 + i, 0:7, :]
        gg[0, at] = full[b * 7, 7, :]
        gs[0, at] = full[b * 7 + 1, 7, :]

    for k in range(7):
        first[k].wait_send()
        last[k].wait_send()
    for t in range(PIECE):

        @pl.when(f != t * 3)
        def _():
            to_owner(t).wait_send()

    @pl.when(owns)
    def _():
        @pl.loop(1, 32)
        def _(k):
            spread(k).wait_send()


def tail(xp, dc, cot, taps, extra):
    vmem = pl.BlockSpec(memory_space=pltpu.VMEM)
    dma = pltpu.SemaphoreType.DMA
    f32, bf16 = jnp.float32, jnp.bfloat16
    return pl.pallas_call(
        tail_kernel,
        out_shape=(
            jax.ShapeDtypeStruct((ROWS, COLS, CHANS), bf16),
            jax.ShapeDtypeStruct((KW, KW, CHANS), f32),
            jax.ShapeDtypeStruct((1, CHANS), f32),
            jax.ShapeDtypeStruct((1, CHANS), f32),
        ),
        in_specs=[vmem] * 5,
        out_specs=(vmem,) * 4,
        scratch_shapes=[
            pltpu.VMEM((NB, PR, PC, 128), f32),
            pltpu.VMEM((3, NB * 16, 128), bf16),
            pltpu.VMEM((3, NB * 16, 128), bf16),
            pltpu.VMEM((88, 8, 128), f32),
            pltpu.VMEM((7, PIECE, 8, 128), f32),
            pltpu.VMEM((PIECE, 8, 128), f32),
            pltpu.VMEM((32, 8, 128), f32),
            pltpu.VMEM((PIECE, 8, 128), f32),
            pltpu.VMEM((88, 8, 128), f32),
            dma((2,)), dma((2,)), dma, dma,
            dma((7,)), dma((7,)), dma((PIECE,)), dma((32,)),
            dma((32,)), dma((PIECE,)), dma((7,)), dma((7,)),
        ],
        compiler_params=pltpu.CompilerParams(
            collective_id=1, has_side_effects=True, vmem_limit_bytes=40 * 2**20
        ),
        name="tail",
    )(xp, dc, cot, taps, extra)


def with_halo(shard, sides, width):
    for axis, dim in sides:
        devices, length = (lax.axis_size(axis), shard.shape[dim])
        up = [(i, (i + 1) % devices) for i in range(devices - 1)]
        down = [(j, i) for i, j in up]
        last = lax.slice_in_dim(shard, length - width, length, axis=dim)
        initial = lax.slice_in_dim(shard, 0, width, axis=dim)
        before = lax.ppermute(last, axis, up)
        after = lax.ppermute(initial, axis, down)
        shard = jnp.concatenate([before, shard, after], axis=dim)
    return shard


def gelu_tanh(v):
    return jax.nn.gelu(v, approximate=True)


def on_device(
    x_code,
    x_exp,
    dw_kernel,
    dw_bias,
    ln_gain,
    ln_bias,
    w_up,
    b_up,
    w_down,
    b_down,
    layer_scale,
    cotangent,
):
    code = x_code[0]
    rows, cols, chans = code.shape
    factor = jnp.exp2(x_exp[0].astype(jnp.float32))
    grouped = code.astype(jnp.float32).reshape(rows, cols, chans // CG, CG) * factor[..., None]
    scaled = grouped.reshape(rows, cols, chans).astype(jnp.bfloat16)
    up_full, down_full = (
        lax.all_gather(w_up, "fsdp", axis=0, tiled=True),
        lax.all_gather(w_down, "fsdp", axis=1, tiled=True),
    )
    padded_x = with_halo(scaled[None], (("sx", 1), ("sy", 2)), 3)[0].astype(jnp.float32)
    conv = jnp.zeros((rows, cols, chans), jnp.float32) + dw_bias
    for i in range(KW):
        for j in range(KW):
            conv = conv + dw_kernel[i, j] * padded_x[i : i + rows, j : j + cols]
    mean_val = jnp.mean(conv, axis=-1, keepdims=True)
    centred = conv - mean_val
    rstd = lax.rsqrt(jnp.mean(centred * centred, axis=-1, keepdims=True) + 1e-06)
    normed = centred * rstd
    ln_out = (normed * ln_gain + ln_bias).astype(jnp.bfloat16).reshape(rows * cols, chans)
    pre = jnp.dot(ln_out, up_full, preferred_element_type=jnp.float32) + b_up
    act, gelu_back = jax.vjp(gelu_tanh, pre)
    mlp = jnp.dot(act.astype(jnp.bfloat16), down_full, preferred_element_type=jnp.float32) + b_down
    mlp = mlp.reshape(rows, cols, chans)
    block_out = (scaled.astype(jnp.float32) + layer_scale * mlp).astype(jnp.bfloat16)
    grad_f = cotangent[0].astype(jnp.float32)
    scale_term = jnp.sum(grad_f * mlp, axis=(0, 1))
    d_mlp = (layer_scale * grad_f).astype(jnp.bfloat16).reshape(rows * cols, chans)
    d_act = lax.dot_general(
        d_mlp, down_full, (((1,), (1,)), ((), ())), preferred_element_type=jnp.float32
    )
    d_pre = gelu_back(d_act)[0].astype(jnp.bfloat16)
    d_ln = lax.dot_general(
        d_pre, up_full, (((1,), (1,)), ((), ())), preferred_element_type=jnp.float32
    )
    d_ln = d_ln.reshape(rows, cols, chans)
    gain_term = jnp.sum(d_ln * normed, axis=(0, 1))
    d_norm = d_ln * ln_gain
    d_conv = rstd * (
        d_norm
        - jnp.mean(d_norm, axis=-1, keepdims=True)
        - normed * jnp.mean(d_norm * normed, axis=-1, keepdims=True)
    )
    blocked_x = padded_x.reshape(rows + 6, cols + 6, NB, 128).transpose(2, 0, 1, 3)
    blocked_x = jnp.pad(blocked_x, ((0, 0), (0, 2), (5, 5), (0, 0)))
    blocked_g = d_conv.reshape(rows, cols, NB, 128).transpose(2, 0, 1, 3)
    grad_input, grad_kernel, grad_gain, grad_scale = tail(
        blocked_x, blocked_g, cotangent[0], dw_kernel, jnp.stack([gain_term, scale_term])
    )
    return (block_out[None], grad_input[None], grad_kernel, grad_gain[0], grad_scale[0])


def solution(mesh):
    placed = (
        P("fsdp", "sx", "sy", None),
        P("fsdp", "sx", "sy", None),
        P(),
        P(),
        P(),
        P(),
        P("fsdp", None),
        P(),
        P(None, "fsdp"),
        P(),
        P(),
        P("fsdp", "sx", "sy", None),
    )
    return jax.shard_map(
        on_device,
        mesh=mesh,
        in_specs=placed,
        out_specs=(P("fsdp", "sx", "sy", None), P("fsdp", "sx", "sy", None), P(), P(), P()),
        check_vma=False,
    )
```

```python
import jax
import jax.numpy as jnp
from jax import lax
from jax.experimental import pallas as pl
from jax.experimental.pallas import tpu as pltpu
from jax.sharding import PartitionSpec as P

CG = 128
KW = 7
NB = 12
ROWS, COLS, CHANS = 8, 16, 1536
PR, PC = 16, 32
PIECE = 11
HID = 1536
GELU_C = 0.7978845608028654
MESH = pl.DeviceIdType.MESH


def remote(src, dst, send, recv, where):
    return pltpu.make_async_remote_copy(
        src_ref=src, dst_ref=dst, send_sem=send, recv_sem=recv, device_id=where, device_id_type=MESH
    )


def row_halo(buf, send, recv, sx, act):
    down = remote(buf.at[:, 8:11, 8:24, :], buf.at[:, 0:3, 8:24, :], send.at[0], recv.at[0], {"sx": sx + 1})
    up = remote(buf.at[:, 3:6, 8:24, :], buf.at[:, 11:14, 8:24, :], send.at[1], recv.at[1], {"sx": sx - 1})
    if act == "start":

        @pl.when(sx < 3)
        def _():
            down.start()

        @pl.when(sx > 0)
        def _():
            up.start()

    else:

        @pl.when(sx < 3)
        def _():
            up.wait_recv()
            down.wait_send()

        @pl.when(sx > 0)
        def _():
            down.wait_recv()
            up.wait_send()


def zero_rows(buf, sx):
    @pl.when(sx == 0)
    def _():
        buf[:, 0:3, :, :] = jnp.zeros((NB, 3, PC, 128), jnp.float32)

    @pl.when(sx == 3)
    def _():
        buf[:, 11:14, :, :] = jnp.zeros((NB, 3, PC, 128), jnp.float32)


def pack_cols(buf, stage, sy):
    for side, first in ((0, 21), (1, 8)):

        @pl.when(sy == side)
        def _():
            @pl.loop(0, NB)
            def _(b):
                for c in range(3):
                    at = pl.multiple_of(b * 16, 16)
                    stage[c, pl.ds(at, 16), :] = buf[b, :, first + c, :].astype(jnp.bfloat16)


def unpack_cols(buf, stage, sy):
    for side, first, other in ((0, 24, 5), (1, 5, 24)):

        @pl.when(sy == side)
        def _():
            @pl.loop(0, NB)
            def _(b):
                for c in range(3):
                    at = pl.multiple_of(b * 16, 16)
                    buf[b, :, first + c, :] = stage[c, pl.ds(at, 16), :].astype(jnp.float32)
                    buf[b, :, other + c, :] = jnp.zeros((PR, 128), jnp.float32)


def lanes(b):
    return pl.ds(pl.multiple_of(b * 128, 128), 128)


def depthwise(buf, b, taps, start, flip):
    acc = start
    for j in range(KW):
        jj = 6 - j if flip else j
        shifted = buf[b, 0:14, 5 + jj : 21 + jj, :]
        for i in range(KW):
            ii = 6 - i if flip else i
            acc = acc + taps[i, j, lanes(b)].reshape(1, 1, 128) * shifted[ii : ii + ROWS]
    return acc


def kernel_grad(xbuf, gbuf, grads, b):
    g = gbuf[b, 3:11, 8:24, :]
    for j in range(KW):
        shifted = xbuf[b, 0:14, 5 + j : 21 + j, :]
        for i in range(KW):
            q = jnp.sum(g * shifted[i : i + ROWS], axis=0)
            grads[b * 7 + i, j, :] = jnp.sum(q, axis=0)


TOK = ROWS * COLS


def block_kernel(
    code, expo, cot, taps, dw_bias, ln_gain, ln_bias, w_up, b_up, w_down, b_down, layer_scale,
    bo, gi, gk, gg, gs,
    xp, gp, stage, landed, up, down, ln, dm, conv, rstd, pre, dact, act, dpre,
    mine_dln, send_dln, got_dln, mine_mlp, send_mlp, got_mlp,
    grads, got1, part, got2, fin, full,
    ls, a1s, a1r, azs, azr, bzs, bzr, bys, byr, bfs, bfr, ts, tr, dls, dlr, mls, mlr,
    hs, hr, cs, cr, s1, r1, s2, r2, s3, r3, s4, r4,
):
    sx, sy, f = lax.axis_index("sx"), lax.axis_index("sy"), lax.axis_index("fsdp")
    g = sx * 2 + sy
    half = lax.rem(sx, 2)
    other = {"sx": sx + 1 - 2 * half}
    z, y = f // 4, lax.rem(f, 4)
    f32, bf16 = jnp.float32, jnp.bfloat16

    def peer(k):
        p = lax.rem(g + k, 8)
        return p, {"sx": p // 2, "sy": lax.rem(p, 2)}

    def zz(d):
        return lax.rem(z + d + 8, 8)

    def yy(d):
        return lax.rem(y + d + 4, 4)

    def shard(buf, dz, dy):
        return buf.at[pl.ds(pl.multiple_of((zz(dz) * 4 + yy(dy)) * 48, 16), 48)]

    def pair(buf, dz, q):
        return buf.at[pl.ds(pl.multiple_of((zz(dz) * 4 + 2 * q) * 48, 16), 96)]

    barrier = pltpu.get_barrier_semaphore()
    for k in range(1, 8):
        pl.semaphore_signal(barrier, inc=1, device_id=peer(k)[1], device_id_type=MESH)

    @pl.loop(1, 32)
    def _(k):
        pl.semaphore_signal(barrier, inc=1, device_id={"fsdp": lax.rem(f + k, 32)}, device_id_type=MESH)

    hidden = pl.ds(pl.multiple_of(half * HID, HID), HID)
    own = [
        pltpu.make_async_copy(w_up.at[:, hidden], shard(up, 0, 0), ls.at[0]),
        pltpu.make_async_copy(w_down.at[:, hidden], shard(down, 0, 0), ls.at[1]),
    ]
    for copy in own:
        copy.start()
    for copy in own:
        copy.wait()
    pl.semaphore_wait(barrier, 38)

    sent = []

    def send(copy):
        copy.start()
        sent.append(copy)

    def up_y(k):
        return remote(shard(up, 0, 0), shard(up, 0, 0), a1s.at[k - 1], a1r.at[k - 1], {"fsdp": z * 4 + yy(k)})

    def up_y_got(k):
        return remote(shard(up, 0, -k), shard(up, 0, -k), a1s.at[k - 1], a1r.at[k - 1], {"fsdp": z * 4 + yy(k)})

    def up_z(way, q, s, got=False):
        sign = 1 - 2 * way
        block = pair(up, -sign * (s if got else s - 1), q)
        at = way * 8 + q * 4 + s - 1
        return remote(block, block, azs.at[at], azr.at[at], {"fsdp": zz(sign) * 4 + y})

    def up_z_steps(s):
        return [(way, q) for way in (0, 1) for q in (0, 1) if s <= (4 if way == q else 3)]

    def down_z(way, s, got=False):
        sign = 1 - 2 * way
        block = shard(down, -sign * (s if got else s - 1), 0)
        at = way * 4 + s - 1
        return remote(block, block, bzs.at[at], bzr.at[at], {"fsdp": zz(sign) * 4 + y})

    def down_y(way, d, got=False):
        sign = 1 - 2 * way
        block = shard(down, d, -sign if got else 0)
        at = way * 8 + d
        return remote(block, block, bys.at[at], byr.at[at], {"fsdp": z * 4 + yy(sign)})

    def down_on(d, got=False):
        sign = 1 - 2 * (d % 2)
        block = shard(down, d, 2 if got else -sign)
        return remote(block, block, bfs.at[d], bfr.at[d], {"fsdp": z * 4 + yy(sign)})

    def step_down_z(s):
        for way in (0, 1):
            if s <= 4 - way:
                down_z(way, s, True).wait_recv()
                if s + 1 <= 4 - way:
                    send(down_z(way, s + 1))
                d = (8 - s) if way == 0 else s
                send(down_y(0, d))
                send(down_y(1, d))

    def step_down_y(d):
        down_y(0, d, True).wait_recv()
        down_y(1, d, True).wait_recv()
        send(down_on(d))

    def step_up_z(s):
        for way, q in up_z_steps(s):
            up_z(way, q, s, True).wait_recv()
            if (way, q) in up_z_steps(s + 1):
                send(up_z(way, q, s + 1))

    for k in (1, 3, 2):
        send(up_y(k))
    send(down_z(0, 1))
    send(down_z(1, 1))
    send(down_y(0, 0))
    send(down_y(1, 0))

    factor = jnp.left_shift(1, expo[...] + 2).astype(f32) * 0.25
    for b in range(NB):
        at = slice(b * 128, (b + 1) * 128)
        scaled = code[:, :, at].astype(f32) * factor[:, :, b : b + 1]
        xp[b, 3:11, 8:24, :] = scaled
    zero_rows(xp, sx)
    row_halo(xp, hs.at[0], hr.at[0], sx, "start")

    @pl.loop(0, NB)
    def _(b):
        ct = cot[:, :, lanes(b)].astype(f32).reshape(TOK, 128)
        dm[0:TOK, lanes(b)] = (layer_scale[:, lanes(b)] * ct).astype(bf16)

    def tokens(buf, at):
        return remote(buf.at[0:TOK], buf.at[TOK : 2 * TOK], ts.at[at], tr.at[at], other)

    send(tokens(dm, 0))

    for k in (1, 3, 2):
        up_y_got(k).wait_recv()
    for way, q in up_z_steps(1):
        send(up_z(way, q, 1))
    step_down_z(1)
    row_halo(xp, hs.at[0], hr.at[0], sx, "wait")
    pack_cols(xp, stage.at[0], sy)
    xcol = remote(stage.at[0], landed.at[0], cs.at[0], cr.at[0], {"sy": 1 - sy})
    xcol.start()
    step_down_y(0)
    zero_rows(gp, sx)
    grads[84:88] = jnp.zeros((4, 8, 128), f32)
    xcol.wait()
    unpack_cols(xp, landed.at[0], sy)

    def forward_conv(b):
        start = jnp.broadcast_to(dw_bias[:, lanes(b)].reshape(1, 1, 128), (ROWS, COLS, 128))
        conv[b] = depthwise(xp, b, taps, start, False).reshape(TOK, 128)

    pl.loop(0, NB)(forward_conv)
    step_down_z(2)

    def over_channels(term):
        total = lax.fori_loop(0, NB, lambda b, t: t + term(b), jnp.zeros((TOK, 128), f32))
        return jnp.sum(total, axis=1, keepdims=True) / CHANS

    mu = over_channels(lambda b: conv[b])
    var = over_channels(lambda b: (conv[b] - mu) * (conv[b] - mu))
    rstd[...] = jnp.broadcast_to(lax.rsqrt(var + 1e-6), (TOK, 128))

    @pl.loop(0, NB)
    def _(b):
        normed = (conv[b] - mu) * rstd[...]
        conv[b] = normed
        ln[0:TOK, lanes(b)] = (normed * ln_gain[:, lanes(b)] + ln_bias[:, lanes(b)]).astype(bf16)

    send(tokens(ln, 1))
    step_down_y(7)
    step_down_y(1)
    step_up_z(1)
    step_down_z(3)
    tokens(dm, 0).wait_recv()
    tokens(ln, 1).wait_recv()

    odd = lax.rem(z, 2)

    def tile(n):
        return pl.ds(pl.multiple_of(n * 256, 256), 256)

    def add_pre(s):
        base = (-odd, -2 + 3 * odd, 2 - 5 * odd, 4 - odd)[s - 1]
        rows = pl.ds(pl.multiple_of(zz(base) * 192, 384), 384)

        @pl.loop(0, 6)
        def _(n):
            term = jnp.dot(ln[:, rows], up[rows, tile(n)], preferred_element_type=f32)
            if s == 1:
                start = pl.multiple_of(half * HID + n * 256, 256)
                pre[:, tile(n)] = term + b_up[:, pl.ds(start, 256)]
            else:
                pre[:, tile(n)] = pre[:, tile(n)] + term

    add_pre(1)
    step_down_y(6)
    step_down_y(2)
    step_up_z(2)
    step_down_z(4)
    add_pre(2)
    step_down_y(5)
    step_down_y(3)
    step_up_z(3)
    step_down_y(4)
    add_pre(3)
    for d in range(8):
        down_on(d, True).wait_recv()

    @pl.loop(0, 6)
    def _(n):
        dact[:, tile(n)] = jnp.dot(dm[...], down[:, tile(n)], preferred_element_type=f32)

    step_up_z(4)
    add_pre(4)

    @pl.loop(0, 12)
    def _(n):
        v = pre[:, lanes(n)]
        v2 = v * v
        t = jnp.tanh(GELU_C * v * (1.0 + 0.044715 * v2))
        cdf = 0.5 * (1.0 + t)
        act[:, lanes(n)] = (v * cdf).astype(bf16)
        slope = cdf + 0.5 * v * (1.0 - t * t) * (GELU_C * (1.0 + 3 * 0.044715 * v2))
        dpre[:, lanes(n)] = (dact[:, lanes(n)] * slope).astype(bf16)

    moved_dln = (send_dln, got_dln, dls, dlr)
    moved_mlp = (send_mlp, got_mlp, mls, mlr)

    def arrived(moved, n):
        src, dst, sends, recvs = moved
        return remote(src.at[:, tile(n)], dst.at[:, tile(n)], sends.at[n], recvs.at[n], other)

    def down_projection(lhs, weights, mine, moved):
        @pl.loop(0, 6)
        def _(n):
            out = lax.dot_general(
                lhs[...], weights[tile(n), :], (((1,), (1,)), ((), ())), preferred_element_type=f32
            )
            mine[:, tile(n)] = out[0:TOK]
            moved[0][:, tile(n)] = out[TOK : 2 * TOK]
            arrived(moved, n).start()

    down_projection(dpre, up, mine_dln, moved_dln)
    down_projection(act, down, mine_mlp, moved_mlp)

    def back_sums(b, sums):
        @pl.when(lax.rem(b, 2) == 0)
        def _():
            arrived(moved_dln, b // 2).wait_recv()

        d_ln = mine_dln[:, lanes(b)] + got_dln[:, lanes(b)]
        grads[b * 7, 7, :] = jnp.sum(d_ln * conv[b], axis=0)
        d_norm = d_ln * ln_gain[:, lanes(b)]
        mine_dln[:, lanes(b)] = d_norm
        return sums[0] + d_norm, sums[1] + d_norm * conv[b]

    zeros = jnp.zeros((TOK, 128), f32)
    sum_d, sum_dn = lax.fori_loop(0, NB, back_sums, (zeros, zeros))
    mean_d = jnp.sum(sum_d, axis=1, keepdims=True) / CHANS
    mean_dn = jnp.sum(sum_dn, axis=1, keepdims=True) / CHANS

    @pl.loop(0, NB)
    def _(b):
        d_conv = rstd[...] * (mine_dln[:, lanes(b)] - mean_d - conv[b] * mean_dn)
        gp[b, 3:11, 8:24, :] = d_conv.reshape(ROWS, COLS, 128)

    row_halo(gp, hs.at[1], hr.at[1], sx, "start")

    @pl.loop(0, NB)
    def _(b):
        @pl.when(lax.rem(b, 2) == 0)
        def _():
            arrived(moved_mlp, b // 2).wait_recv()

        mlp = (mine_mlp[:, lanes(b)] + got_mlp[:, lanes(b)]) + b_down[:, lanes(b)]
        ct = cot[:, :, lanes(b)].astype(jnp.float32).reshape(TOK, 128)
        grads[b * 7 + 1, 7, :] = jnp.sum(ct * mlp, axis=0)
        scaled = xp[b, 3:11, 8:24, :].reshape(TOK, 128)
        bo[:, lanes(b)] = (scaled + layer_scale[:, lanes(b)] * mlp).astype(jnp.bfloat16)
        for i in range(2, 7):
            grads[b * 7 + i, 7, :] = jnp.zeros((128,), jnp.float32)

    @pl.loop(0, 6)
    def _(b):
        kernel_grad(xp, gp, grads, b)

    row_halo(gp, hs.at[1], hr.at[1], sx, "wait")
    pack_cols(gp, stage.at[1], sy)
    col = remote(stage.at[1], landed.at[1], cs.at[1], cr.at[1], {"sy": 1 - sy})
    col.start()

    @pl.loop(6, NB)
    def _(b):
        kernel_grad(xp, gp, grads, b)

    first = []
    for k in range(1, 8):
        p, where = peer(k)
        first.append(remote(grads.at[pl.ds(p * PIECE, PIECE)], got1.at[k - 1], s1.at[k - 1], r1.at[k - 1], where))
        first[-1].start()

    col.wait()
    unpack_cols(gp, landed.at[1], sy)

    def out_conv(b):
        gi[:, :, lanes(b)] = depthwise(
            gp, b, taps, cot[:, :, lanes(b)].astype(jnp.float32), True
        ).astype(jnp.bfloat16)

    pl.loop(0, 4)(out_conv)

    total = grads[pl.ds(g * PIECE, PIECE)]
    for k in range(7):
        first[k].wait_recv()
        total = total + got1[k]
    part[...] = total

    def to_owner(t):
        owner = t * 3
        slot = lax.rem(f - owner + 32, 32)
        return remote(part.at[t], got2.at[slot], s2.at[t], r2.at[slot], {"fsdp": owner})

    for t in range(PIECE):

        @pl.when(f != t * 3)
        def _():
            to_owner(t).start()

    pl.loop(4, 8)(out_conv)

    mine = f // 3
    owns = lax.rem(f, 3) == 0

    def spread(k):
        return remote(fin.at[mine], fin.at[mine], s3.at[k], r3.at[mine], {"fsdp": lax.rem(f + k, 32)})

    @pl.when(owns)
    def _():
        fin[mine] = part[mine]

        @pl.loop(1, 32)
        def _(k):
            remote(part.at[0], got2.at[k], s2.at[0], r2.at[k], {"fsdp": f}).wait_recv()
            fin[mine] = fin[mine] + got2[k]

        @pl.loop(1, 32)
        def _(k):
            spread(k).start()

    pl.loop(8, NB)(out_conv)

    for t in range(PIECE):

        @pl.when(f != t * 3)
        def _():
            remote(fin.at[t], fin.at[t], s3.at[0], r3.at[t], {"fsdp": t * 3}).wait_recv()

    last = []
    for k in range(1, 8):
        p, where = peer(k)
        last.append(remote(fin, full.at[pl.ds(g * PIECE, PIECE)], s4.at[k - 1], r4.at[k - 1], where))
        last[-1].start()
    full[pl.ds(g * PIECE, PIECE)] = fin[...]
    for k in range(7):
        last[k].wait_recv()
    for b in range(NB):
        at = slice(b * 128, (b + 1) * 128)
        for i in range(KW):
            gk[i, :, at] = full[b * 7 + i, 0:7, :]
        gg[0, at] = full[b * 7, 7, :]
        gs[0, at] = full[b * 7 + 1, 7, :]

    for k in range(7):
        first[k].wait_send()
        last[k].wait_send()
    for t in range(PIECE):

        @pl.when(f != t * 3)
        def _():
            to_owner(t).wait_send()

    @pl.when(owns)
    def _():
        @pl.loop(1, 32)
        def _(k):
            spread(k).wait_send()

    for n in range(6):
        arrived(moved_dln, n).wait_send()
        arrived(moved_mlp, n).wait_send()
    for copy in sent:
        copy.wait_send()


def on_device(
    x_code, x_exp, dw_kernel, dw_bias, ln_gain, ln_bias, w_up, b_up, w_down, b_down, layer_scale, cotangent
):
    vmem = pl.BlockSpec(memory_space=pltpu.VMEM)
    anywhere = pl.BlockSpec(memory_space=pl.ANY)
    dma = pltpu.SemaphoreType.DMA
    f32, bf16 = jnp.float32, jnp.bfloat16
    row = lambda v: v.reshape(1, -1)
    tok_f32 = pltpu.VMEM((TOK, CHANS), f32)
    pair_f32, pair_bf16 = pltpu.VMEM((2 * TOK, HID), f32), pltpu.VMEM((2 * TOK, HID), bf16)
    weight = pltpu.VMEM((CHANS, HID), bf16)
    padded = pltpu.VMEM((NB, PR, PC, 128), f32)
    staged = pltpu.VMEM((2, 3, NB * 16, 128), bf16)
    block_out, grad_input, grad_kernel, grad_gain, grad_scale = pl.pallas_call(
        block_kernel,
        out_shape=(
            jax.ShapeDtypeStruct((TOK, CHANS), bf16),
            jax.ShapeDtypeStruct((ROWS, COLS, CHANS), bf16),
            jax.ShapeDtypeStruct((KW, KW, CHANS), f32),
            jax.ShapeDtypeStruct((1, CHANS), f32),
            jax.ShapeDtypeStruct((1, CHANS), f32),
        ),
        in_specs=[vmem] * 7 + [anywhere, vmem, anywhere, vmem, vmem],
        out_specs=(vmem,) * 5,
        scratch_shapes=[
            padded, padded, staged, staged, weight, weight, pair_bf16, pair_bf16,
            pltpu.VMEM((NB, TOK, 128), f32), pltpu.VMEM((TOK, 128), f32),
            pair_f32, pair_f32, pair_bf16, pair_bf16,
            tok_f32, tok_f32, tok_f32, tok_f32, tok_f32, tok_f32,
            pltpu.VMEM((88, 8, 128), f32),
            pltpu.VMEM((7, PIECE, 8, 128), f32),
            pltpu.VMEM((PIECE, 8, 128), f32),
            pltpu.VMEM((32, 8, 128), f32),
            pltpu.VMEM((PIECE, 8, 128), f32),
            pltpu.VMEM((88, 8, 128), f32),
            dma((2,)), dma((3,)), dma((3,)), dma((16,)), dma((16,)), dma((8,)), dma((8,)),
            dma((16,)), dma((16,)), dma((8,)), dma((8,)), dma((2,)), dma((2,)),
            dma((6,)), dma((6,)), dma((6,)), dma((6,)),
            dma((2, 2)), dma((2, 2)), dma((2,)), dma((2,)),
            dma((7,)), dma((7,)), dma((PIECE,)), dma((32,)),
            dma((32,)), dma((PIECE,)), dma((7,)), dma((7,)),
        ],
        compiler_params=pltpu.CompilerParams(
            collective_id=1, has_side_effects=True, vmem_limit_bytes=56 * 2**20
        ),
        name="block",
    )(
        x_code[0], x_exp[0], cotangent[0], dw_kernel, row(dw_bias), row(ln_gain), row(ln_bias),
        w_up, row(b_up), w_down.T, row(b_down), row(layer_scale),
    )
    return (
        block_out.reshape(1, ROWS, COLS, CHANS), grad_input[None], grad_kernel, grad_gain[0], grad_scale[0]
    )


def solution(mesh):
    placed = (
        P("fsdp", "sx", "sy", None),
        P("fsdp", "sx", "sy", None),
        P(),
        P(),
        P(),
        P(),
        P("fsdp", None),
        P(),
        P(None, "fsdp"),
        P(),
        P(),
        P("fsdp", "sx", "sy", None),
    )
    return jax.shard_map(
        on_device,
        mesh=mesh,
        in_specs=placed,
        out_specs=(P("fsdp", "sx", "sy", None), P("fsdp", "sx", "sy", None), P(), P(), P()),
        check_vma=False,
    )
```

```python
import jax
import jax.numpy as jnp
from jax import lax
from jax.experimental import pallas as pl
from jax.experimental.pallas import tpu as pltpu
from jax.sharding import PartitionSpec as P

CG = 128
KW = 7
NB = 12
ROWS, COLS, CHANS = 8, 16, 1536
PR, PC = 16, 32
PIECE = 11
HID = 1536
GELU_C = 0.7978845608028654
MESH = pl.DeviceIdType.MESH


def remote(src, dst, send, recv, where):
    return pltpu.make_async_remote_copy(
        src_ref=src, dst_ref=dst, send_sem=send, recv_sem=recv, device_id=where, device_id_type=MESH
    )


def row_halo(buf, send, recv, sx, act):
    down = remote(buf.at[:, 8:11, 8:24, :], buf.at[:, 0:3, 8:24, :], send.at[0], recv.at[0], {"sx": sx + 1})
    up = remote(buf.at[:, 3:6, 8:24, :], buf.at[:, 11:14, 8:24, :], send.at[1], recv.at[1], {"sx": sx - 1})
    if act == "start":

        @pl.when(sx < 3)
        def _():
            down.start()

        @pl.when(sx > 0)
        def _():
            up.start()

    else:

        @pl.when(sx < 3)
        def _():
            up.wait_recv()
            down.wait_send()

        @pl.when(sx > 0)
        def _():
            down.wait_recv()
            up.wait_send()


def zero_rows(buf, sx):
    @pl.when(sx == 0)
    def _():
        buf[:, 0:3, :, :] = jnp.zeros((NB, 3, PC, 128), jnp.float32)

    @pl.when(sx == 3)
    def _():
        buf[:, 11:14, :, :] = jnp.zeros((NB, 3, PC, 128), jnp.float32)


def pack_cols(buf, stage, sy):
    for side, first in ((0, 21), (1, 8)):

        @pl.when(sy == side)
        def _():
            @pl.loop(0, NB)
            def _(b):
                for c in range(3):
                    at = pl.multiple_of(b * 16, 16)
                    stage[c, pl.ds(at, 16), :] = buf[b, :, first + c, :].astype(jnp.bfloat16)


def unpack_cols(buf, stage, sy):
    for side, first, other in ((0, 24, 5), (1, 5, 24)):

        @pl.when(sy == side)
        def _():
            @pl.loop(0, NB)
            def _(b):
                for c in range(3):
                    at = pl.multiple_of(b * 16, 16)
                    buf[b, :, first + c, :] = stage[c, pl.ds(at, 16), :].astype(jnp.float32)
                    buf[b, :, other + c, :] = jnp.zeros((PR, 128), jnp.float32)


def lanes(b):
    return pl.ds(pl.multiple_of(b * 128, 128), 128)


def depthwise(buf, b, taps, start, flip):
    acc = start
    for j in range(KW):
        jj = 6 - j if flip else j
        shifted = buf[b, 0:14, 5 + jj : 21 + jj, :]
        for i in range(KW):
            ii = 6 - i if flip else i
            acc = acc + taps[i, j, lanes(b)].reshape(1, 1, 128) * shifted[ii : ii + ROWS]
    return acc


def kernel_grad(xbuf, gbuf, grads, b):
    g = gbuf[b, 3:11, 8:24, :]
    for j in range(KW):
        shifted = xbuf[b, 0:14, 5 + j : 21 + j, :]
        for i in range(KW):
            q = jnp.sum(g * shifted[i : i + ROWS], axis=0)
            grads[b * 7 + i, j, :] = jnp.sum(q, axis=0)


TOK = ROWS * COLS


def block_kernel(
    code, expo, cot, taps, dw_bias_in, ln_gain_in, ln_bias_in, w_up, b_up, w_down, b_down_in, layer_scale_in,
    bo, gi, gk, gg, gs,
    dw_bias, ln_gain, ln_bias, b_down, layer_scale, xp, gp, stage, landed, up, down, ln, dm, conv, rstd, pre, dact, act, dpre,
    mine_dln, send_dln, got_dln, mine_mlp, send_mlp, got_mlp,
    grads, got1, part, got2, fin, full,
    ls, vs, xus, xur, xds, xdr, a1s, a1r, azs, azr, bzs, bzr, bys, byr, bfs, bfr, ts, tr, dls, dlr, mls, mlr,
    hs, hr, cs, cr, s1, r1, s2, r2, s3, r3, s4, r4,
):
    sx, sy, f = lax.axis_index("sx"), lax.axis_index("sy"), lax.axis_index("fsdp")
    g = sx * 2 + sy
    half = lax.rem(sx, 2)
    other = {"sx": sx + 1 - 2 * half}
    z, y = f // 4, lax.rem(f, 4)
    f32, bf16 = jnp.float32, jnp.bfloat16

    def peer(k):
        p = lax.rem(g + k, 8)
        return p, {"sx": p // 2, "sy": lax.rem(p, 2)}

    x = sy * 2 + sx // 2
    odd_x = lax.rem(x, 2)
    window = pl.ds(pl.multiple_of(odd_x * 512, 512), 1024)

    def x_peer(sign):
        to = lax.rem(x + sign + 4, 4)
        return {"sx": lax.rem(to, 2) * 2 + half, "sy": to // 2}

    def zz(d):
        return lax.rem(z + d + 8, 8)

    def yy(d):
        return lax.rem(y + d + 4, 4)

    def shard(buf, dz, dy):
        return buf.at[pl.ds(pl.multiple_of((zz(dz) * 4 + yy(dy)) * 48, 16), 48), window]

    def pair(buf, dz, q):
        return buf.at[pl.ds(pl.multiple_of((zz(dz) * 4 + 2 * q) * 48, 16), 96), window]

    barrier = pltpu.get_barrier_semaphore()
    near = [{"fsdp": zz(1) * 4 + y}, {"fsdp": zz(-1) * 4 + y}]
    near += [{"fsdp": z * 4 + yy(k)} for k in (1, 2, 3)] + [peer(k)[1] for k in range(1, 8)]
    for where in near:
        pl.semaphore_signal(barrier, inc=1, device_id=where, device_id_type=MESH)

    mine = pl.ds(pl.multiple_of(half * HID + odd_x * 512, 512), 1024)
    own = [
        pltpu.make_async_copy(w_up.at[:, mine], shard(up, 0, 0), ls.at[0]),
        pltpu.make_async_copy(w_down.at[:, mine], shard(down, 0, 0), ls.at[1]),
    ]
    vectors = (
        (dw_bias_in, dw_bias), (ln_gain_in, ln_gain), (ln_bias_in, ln_bias), (b_down_in, b_down),
        (layer_scale_in, layer_scale),
    )
    rows_in = [pltpu.make_async_copy(src, dst.at[0], vs.at[n]) for n, (src, dst) in enumerate(vectors)]
    for copy in own + rows_in:
        copy.start()
    for copy in own:
        copy.wait()
    pl.semaphore_wait(barrier, len(near))

    sent = []

    def send(copy):
        copy.start()
        sent.append(copy)

    def up_y(k):
        return remote(shard(up, 0, 0), shard(up, 0, 0), a1s.at[k - 1], a1r.at[k - 1], {"fsdp": z * 4 + yy(k)})

    def up_y_got(k):
        return remote(shard(up, 0, -k), shard(up, 0, -k), a1s.at[k - 1], a1r.at[k - 1], {"fsdp": z * 4 + yy(k)})

    def up_z(way, q, s, got=False):
        sign = 1 - 2 * way
        block = pair(up, -sign * (s if got else s - 1), q)
        at = way * 8 + q * 4 + s - 1
        return remote(block, block, azs.at[at], azr.at[at], {"fsdp": zz(sign) * 4 + y})

    def up_z_steps(s):
        return [(way, q) for way in (0, 1) for q in (0, 1) if s <= (4 if way == q else 3)]

    def down_z(way, s, got=False):
        sign = 1 - 2 * way
        block = shard(down, -sign * (s if got else s - 1), 0)
        at = way * 4 + s - 1
        return remote(block, block, bzs.at[at], bzr.at[at], {"fsdp": zz(sign) * 4 + y})

    def down_y(way, d, got=False):
        sign = 1 - 2 * way
        block = shard(down, d, -sign if got else 0)
        at = way * 8 + d
        return remote(block, block, bys.at[at], byr.at[at], {"fsdp": z * 4 + yy(sign)})

    def down_on(d, got=False):
        sign = 1 - 2 * (d % 2)
        block = shard(down, d, 2 if got else -sign)
        return remote(block, block, bfs.at[d], bfr.at[d], {"fsdp": z * 4 + yy(sign)})

    def x_send(buf, d, got=False):
        sends, recvs = (xus, xur) if buf is up else (xds, xdr)
        rows = pl.ds(pl.multiple_of(zz(d) * 192, 16), 192)
        copies = []
        for way in (0, 1):
            third = (1 - odd_x if got else odd_x) * 1024 + way * 256
            block = buf.at[rows, pl.ds(pl.multiple_of(third, 256), 256)]
            at = way * 8 + d % 8
            copies.append(remote(block, block, sends.at[at], recvs.at[at], x_peer(1 - 2 * way)))
        return copies

    def x_forward(buf, d):
        for copy in x_send(buf, d):
            send(copy)

    def x_arrived(buf, d):
        for copy in x_send(buf, d, True):
            copy.wait_recv()

    def step_down_on(d):
        down_on(d, True).wait_recv()
        x_forward(down, d)

    def step_down_z(s):
        for way in (0, 1):
            if s <= 4 - way:
                down_z(way, s, True).wait_recv()
                if s + 1 <= 4 - way:
                    send(down_z(way, s + 1))
                d = (8 - s) if way == 0 else s
                send(down_y(0, d))
                send(down_y(1, d))

    def step_down_y(d):
        down_y(0, d, True).wait_recv()
        down_y(1, d, True).wait_recv()
        send(down_on(d))

    def step_up_z(s):
        for way, q in up_z_steps(s):
            up_z(way, q, s, True).wait_recv()
            if (way, q) in up_z_steps(s + 1):
                send(up_z(way, q, s + 1))
        for d in (-s, s) if s < 4 else (4,):
            x_forward(up, d)

    for k in (1, 3, 2):
        send(up_y(k))
    send(down_z(0, 1))
    send(down_z(1, 1))
    send(down_y(0, 0))
    send(down_y(1, 0))

    factor = jnp.left_shift(1, expo[...] + 2).astype(f32) * 0.25
    for b in range(NB):
        at = slice(b * 128, (b + 1) * 128)
        scaled = code[:, :, at].astype(f32) * factor[:, :, b : b + 1]
        xp[b, 3:11, 8:24, :] = scaled
    zero_rows(xp, sx)
    row_halo(xp, hs.at[0], hr.at[0], sx, "start")

    step_down_z(1)
    for copy in rows_in:
        copy.wait()

    @pl.loop(0, NB)
    def _(b):
        ct = cot[:, :, lanes(b)].astype(f32).reshape(TOK, 128)
        dm[0:TOK, lanes(b)] = (layer_scale[:, lanes(b)] * ct).astype(bf16)

    def tokens(buf, at):
        return remote(buf.at[0:TOK], buf.at[TOK : 2 * TOK], ts.at[at], tr.at[at], other)

    send(tokens(dm, 0))

    for k in (1, 3, 2):
        up_y_got(k).wait_recv()
    for way, q in up_z_steps(1):
        send(up_z(way, q, 1))
    x_forward(up, 0)
    row_halo(xp, hs.at[0], hr.at[0], sx, "wait")
    pack_cols(xp, stage.at[0], sy)
    xcol = remote(stage.at[0], landed.at[0], cs.at[0], cr.at[0], {"sy": 1 - sy})
    xcol.start()
    step_down_z(2)
    step_down_y(0)
    zero_rows(gp, sx)
    grads[84:88] = jnp.zeros((4, 8, 128), f32)
    step_down_z(3)
    step_down_y(7)
    step_down_y(1)
    step_down_on(0)
    xcol.wait()
    unpack_cols(xp, landed.at[0], sy)

    def forward_conv(b):
        start = jnp.broadcast_to(dw_bias[:, lanes(b)].reshape(1, 1, 128), (ROWS, COLS, 128))
        conv[b] = depthwise(xp, b, taps, start, False).reshape(TOK, 128)

    pl.loop(0, 4)(forward_conv)
    step_up_z(1)
    pl.loop(4, 8)(forward_conv)
    step_down_z(4)
    step_down_y(6)
    step_down_y(2)
    pl.loop(8, NB)(forward_conv)
    step_down_on(7)
    step_down_on(1)

    def over_channels(term):
        total = lax.fori_loop(0, NB, lambda b, t: t + term(b), jnp.zeros((TOK, 128), f32))
        return jnp.sum(total, axis=1, keepdims=True) / CHANS

    mu = over_channels(lambda b: conv[b])
    var = over_channels(lambda b: (conv[b] - mu) * (conv[b] - mu))
    rstd[...] = jnp.broadcast_to(lax.rsqrt(var + 1e-6), (TOK, 128))

    @pl.loop(0, NB)
    def _(b):
        normed = (conv[b] - mu) * rstd[...]
        conv[b] = normed
        ln[0:TOK, lanes(b)] = (normed * ln_gain[:, lanes(b)] + ln_bias[:, lanes(b)]).astype(bf16)

    send(tokens(ln, 1))
    step_down_y(5)
    step_down_y(3)
    step_up_z(2)
    tokens(dm, 0).wait_recv()
    tokens(ln, 1).wait_recv()

    odd = lax.rem(z, 2)

    def tile(n):
        return pl.ds(pl.multiple_of(n * 256, 256), 256)

    def add_pre(s):
        base = (-odd, -2 + 3 * odd, 2 - 5 * odd, 4 - odd)[s - 1]
        rows = pl.ds(pl.multiple_of(zz(base) * 192, 384), 384)

        @pl.loop(0, 6)
        def _(n):
            term = jnp.dot(ln[:, rows], up[rows, tile(n)], preferred_element_type=f32)
            if s == 1:
                start = pl.multiple_of(half * HID + n * 256, 256)
                pre[:, tile(n)] = term + b_up[:, pl.ds(start, 256)]
            else:
                pre[:, tile(n)] = pre[:, tile(n)] + term

    step_down_on(6)
    step_down_on(2)
    step_down_y(4)
    for d in (0, -1, 1):
        x_arrived(up, d)
    add_pre(1)
    step_up_z(3)
    step_down_on(5)
    step_down_on(3)
    for d in (-2, 2):
        x_arrived(up, d)
    add_pre(2)
    step_down_on(4)
    step_up_z(4)
    for d in (-3, 3):
        x_arrived(up, d)
    add_pre(3)
    for d in range(8):
        x_arrived(down, d)

    @pl.loop(0, 6)
    def _(n):
        dact[:, tile(n)] = jnp.dot(dm[...], down[:, tile(n)], preferred_element_type=f32)

    x_arrived(up, 4)
    add_pre(4)

    @pl.loop(0, 12)
    def _(n):
        v = pre[:, lanes(n)]
        v2 = v * v
        t = jnp.tanh(GELU_C * v * (1.0 + 0.044715 * v2))
        cdf = 0.5 * (1.0 + t)
        act[:, lanes(n)] = (v * cdf).astype(bf16)
        slope = cdf + 0.5 * v * (1.0 - t * t) * (GELU_C * (1.0 + 3 * 0.044715 * v2))
        dpre[:, lanes(n)] = (dact[:, lanes(n)] * slope).astype(bf16)

    moved_dln = (send_dln, got_dln, dls, dlr)
    moved_mlp = (send_mlp, got_mlp, mls, mlr)

    def arrived(moved, n):
        src, dst, sends, recvs = moved
        return remote(src.at[:, tile(n)], dst.at[:, tile(n)], sends.at[n], recvs.at[n], other)

    def down_projection(lhs, weights, mine, moved):
        @pl.loop(0, 6)
        def _(n):
            out = lax.dot_general(
                lhs[...], weights[tile(n), :], (((1,), (1,)), ((), ())), preferred_element_type=f32
            )
            mine[:, tile(n)] = out[0:TOK]
            moved[0][:, tile(n)] = out[TOK : 2 * TOK]
            arrived(moved, n).start()

    down_projection(dpre, up, mine_dln, moved_dln)
    down_projection(act, down, mine_mlp, moved_mlp)

    def back_sums(b, sums):
        @pl.when(lax.rem(b, 2) == 0)
        def _():
            arrived(moved_dln, b // 2).wait_recv()

        d_ln = mine_dln[:, lanes(b)] + got_dln[:, lanes(b)]
        grads[b * 7, 7, :] = jnp.sum(d_ln * conv[b], axis=0)
        d_norm = d_ln * ln_gain[:, lanes(b)]
        mine_dln[:, lanes(b)] = d_norm
        return sums[0] + d_norm, sums[1] + d_norm * conv[b]

    zeros = jnp.zeros((TOK, 128), f32)
    sum_d, sum_dn = lax.fori_loop(0, NB, back_sums, (zeros, zeros))
    mean_d = jnp.sum(sum_d, axis=1, keepdims=True) / CHANS
    mean_dn = jnp.sum(sum_dn, axis=1, keepdims=True) / CHANS

    @pl.loop(0, NB)
    def _(b):
        d_conv = rstd[...] * (mine_dln[:, lanes(b)] - mean_d - conv[b] * mean_dn)
        gp[b, 3:11, 8:24, :] = d_conv.reshape(ROWS, COLS, 128)

    row_halo(gp, hs.at[1], hr.at[1], sx, "start")

    @pl.loop(0, NB)
    def _(b):
        @pl.when(lax.rem(b, 2) == 0)
        def _():
            arrived(moved_mlp, b // 2).wait_recv()

        mlp = (mine_mlp[:, lanes(b)] + got_mlp[:, lanes(b)]) + b_down[:, lanes(b)]
        ct = cot[:, :, lanes(b)].astype(jnp.float32).reshape(TOK, 128)
        grads[b * 7 + 1, 7, :] = jnp.sum(ct * mlp, axis=0)
        scaled = xp[b, 3:11, 8:24, :].reshape(TOK, 128)
        bo[:, lanes(b)] = (scaled + layer_scale[:, lanes(b)] * mlp).astype(jnp.bfloat16)
        for i in range(2, 7):
            grads[b * 7 + i, 7, :] = jnp.zeros((128,), jnp.float32)

    @pl.loop(0, 6)
    def _(b):
        kernel_grad(xp, gp, grads, b)

    row_halo(gp, hs.at[1], hr.at[1], sx, "wait")
    pack_cols(gp, stage.at[1], sy)
    col = remote(stage.at[1], landed.at[1], cs.at[1], cr.at[1], {"sy": 1 - sy})
    col.start()

    @pl.loop(6, NB)
    def _(b):
        kernel_grad(xp, gp, grads, b)

    first = []
    for k in range(1, 8):
        p, where = peer(k)
        first.append(remote(grads.at[pl.ds(p * PIECE, PIECE)], got1.at[k - 1], s1.at[k - 1], r1.at[k - 1], where))
        first[-1].start()

    col.wait()
    unpack_cols(gp, landed.at[1], sy)

    def out_conv(b):
        gi[:, :, lanes(b)] = depthwise(
            gp, b, taps, cot[:, :, lanes(b)].astype(jnp.float32), True
        ).astype(jnp.bfloat16)

    pl.loop(0, 4)(out_conv)

    total = grads[pl.ds(g * PIECE, PIECE)]
    for k in range(7):
        first[k].wait_recv()
        total = total + got1[k]
    part[...] = total

    def to_owner(t):
        owner = t * 3
        slot = lax.rem(f - owner + 32, 32)
        return remote(part.at[t], got2.at[slot], s2.at[t], r2.at[slot], {"fsdp": owner})

    for t in range(PIECE):

        @pl.when(f != t * 3)
        def _():
            to_owner(t).start()

    pl.loop(4, 8)(out_conv)

    mine = f // 3
    owns = lax.rem(f, 3) == 0

    def spread(k):
        return remote(fin.at[mine], fin.at[mine], s3.at[k], r3.at[mine], {"fsdp": lax.rem(f + k, 32)})

    @pl.when(owns)
    def _():
        fin[mine] = part[mine]

        @pl.loop(1, 32)
        def _(k):
            remote(part.at[0], got2.at[k], s2.at[0], r2.at[k], {"fsdp": f}).wait_recv()
            fin[mine] = fin[mine] + got2[k]

        @pl.loop(1, 32)
        def _(k):
            spread(k).start()

    pl.loop(8, NB)(out_conv)

    for t in range(PIECE):

        @pl.when(f != t * 3)
        def _():
            remote(fin.at[t], fin.at[t], s3.at[0], r3.at[t], {"fsdp": t * 3}).wait_recv()

    last = []
    for k in range(1, 8):
        p, where = peer(k)
        last.append(remote(fin, full.at[pl.ds(g * PIECE, PIECE)], s4.at[k - 1], r4.at[k - 1], where))
        last[-1].start()
    full[pl.ds(g * PIECE, PIECE)] = fin[...]
    for k in range(7):
        last[k].wait_recv()
    for b in range(NB):
        at = slice(b * 128, (b + 1) * 128)
        for i in range(KW):
            gk[i, :, at] = full[b * 7 + i, 0:7, :]
        gg[at] = full[b * 7, 7, :]
        gs[at] = full[b * 7 + 1, 7, :]

    for k in range(7):
        first[k].wait_send()
        last[k].wait_send()
    for t in range(PIECE):

        @pl.when(f != t * 3)
        def _():
            to_owner(t).wait_send()

    @pl.when(owns)
    def _():
        @pl.loop(1, 32)
        def _(k):
            spread(k).wait_send()

    for n in range(6):
        arrived(moved_dln, n).wait_send()
        arrived(moved_mlp, n).wait_send()
    for copy in sent:
        copy.wait_send()


def on_device(
    x_code, x_exp, dw_kernel, dw_bias, ln_gain, ln_bias, w_up, b_up, w_down, b_down, layer_scale, cotangent
):
    vmem = pl.BlockSpec(memory_space=pltpu.VMEM)
    anywhere = pl.BlockSpec(memory_space=pl.ANY)
    dma = pltpu.SemaphoreType.DMA
    f32, bf16 = jnp.float32, jnp.bfloat16
    row = lambda v: v.reshape(1, -1)
    tok_f32 = pltpu.VMEM((TOK, CHANS), f32)
    pair_f32, pair_bf16 = pltpu.VMEM((2 * TOK, HID), f32), pltpu.VMEM((2 * TOK, HID), bf16)
    weight = pltpu.VMEM((CHANS, HID), bf16)
    padded = pltpu.VMEM((NB, PR, PC, 128), f32)
    staged = pltpu.VMEM((2, 3, NB * 16, 128), bf16)
    block_out, grad_input, grad_kernel, grad_gain, grad_scale = pl.pallas_call(
        block_kernel,
        out_shape=(
            jax.ShapeDtypeStruct((TOK, CHANS), bf16),
            jax.ShapeDtypeStruct((ROWS, COLS, CHANS), bf16),
            jax.ShapeDtypeStruct((KW, KW, CHANS), f32),
            jax.ShapeDtypeStruct((CHANS,), f32),
            jax.ShapeDtypeStruct((CHANS,), f32),
        ),
        in_specs=[vmem] * 4 + [anywhere] * 4 + [vmem] + [anywhere] * 3,
        out_specs=(vmem,) * 5,
        scratch_shapes=[
            *[pltpu.VMEM((1, CHANS), f32)] * 5, padded, padded, staged, staged, weight, weight, pair_bf16, pair_bf16,
            pltpu.VMEM((NB, TOK, 128), f32), pltpu.VMEM((TOK, 128), f32),
            pair_f32, pair_f32, pair_bf16, pair_bf16,
            tok_f32, tok_f32, tok_f32, tok_f32, tok_f32, tok_f32,
            pltpu.VMEM((88, 8, 128), f32),
            pltpu.VMEM((7, PIECE, 8, 128), f32),
            pltpu.VMEM((PIECE, 8, 128), f32),
            pltpu.VMEM((32, 8, 128), f32),
            pltpu.VMEM((PIECE, 8, 128), f32),
            pltpu.VMEM((88, 8, 128), f32),
            dma((2,)), dma((5,)), dma((16,)), dma((16,)), dma((16,)), dma((16,)),
            dma((3,)), dma((3,)), dma((16,)), dma((16,)), dma((8,)), dma((8,)),
            dma((16,)), dma((16,)), dma((8,)), dma((8,)), dma((2,)), dma((2,)),
            dma((6,)), dma((6,)), dma((6,)), dma((6,)),
            dma((2, 2)), dma((2, 2)), dma((2,)), dma((2,)),
            dma((7,)), dma((7,)), dma((PIECE,)), dma((32,)),
            dma((32,)), dma((PIECE,)), dma((7,)), dma((7,)),
        ],
        compiler_params=pltpu.CompilerParams(
            collective_id=1, has_side_effects=True, vmem_limit_bytes=56 * 2**20
        ),
        name="block",
    )(
        x_code[0], x_exp[0], cotangent[0], dw_kernel, dw_bias, ln_gain, ln_bias,
        w_up, row(b_up), w_down.T, b_down, layer_scale,
    )
    return (
        block_out.reshape(1, ROWS, COLS, CHANS), grad_input[None], grad_kernel, grad_gain, grad_scale
    )


def solution(mesh):
    placed = (
        P("fsdp", "sx", "sy", None),
        P("fsdp", "sx", "sy", None),
        P(),
        P(),
        P(),
        P(),
        P("fsdp", None),
        P(),
        P(None, "fsdp"),
        P(),
        P(),
        P("fsdp", "sx", "sy", None),
    )
    return jax.shard_map(
        on_device,
        mesh=mesh,
        in_specs=placed,
        out_specs=(P("fsdp", "sx", "sy", None), P("fsdp", "sx", "sy", None), P(), P(), P()),
        check_vma=False,
    )
```

```python
import jax
import jax.numpy as jnp
from jax import lax
from jax.experimental import pallas as pl
from jax.experimental.pallas import tpu as pltpu
from jax.sharding import PartitionSpec as P

CG = 128
KW = 7
NB = 12
ROWS, COLS, CHANS = 8, 16, 1536
PR, PC = 16, 32
PIECE = 11
HID = 1536
MISSING_UP, MISSING_DOWN = 640, 512
ORDER = (
    ("uz", 0, 0, 1), ("uz", 1, 0, 1), ("uy", 1), ("uy", 3), ("uy", 2), ("tokens",), ("dz", 0, 1),
    ("dz", 1, 1), ("dy", 0, 0), ("dy", 1, 0), ("xcols",), ("uz", 0, 0, 2), ("uz", 1, 0, 2), ("dy", 0, 7),
    ("dy", 1, 7), ("uz", 0, 1, 1), ("uz", 1, 1, 1), ("uz", 0, 3, 1), ("uz", 1, 3, 1), ("dy", 0, 1),
    ("dy", 1, 1), ("do", 0), ("dz", 0, 2), ("dz", 1, 2), ("uz", 0, 2, 1), ("uz", 1, 2, 1), ("unpack",),
    ("conv", 0), ("do", 7), ("dy", 0, 6), ("uz", 0, 0, 3), ("uz", 1, 0, 3), ("conv", 3), ("do", 1),
    ("dy", 1, 6), ("dy", 0, 2), ("uz", 0, 1, 2), ("uz", 1, 1, 2), ("conv", 6), ("dz", 0, 3), ("dz", 1, 3),
    ("dy", 1, 2), ("uz", 0, 3, 2), ("uz", 1, 3, 2), ("conv", 9), ("do", 6), ("norm",), ("dy", 1, 5),
    ("uz", 0, 2, 2), ("uz", 1, 2, 2), ("do", 2), ("dy", 0, 5), ("dy", 1, 3), ("uz", 0, 0, 4),
    ("uz", 1, 1, 3), ("back", 1), ("dz", 0, 4), ("dy", 0, 3), ("uz", 0, 1, 3), ("uz", 1, 3, 3), ("pre", 1),
    ("uz", 1, 2, 3), ("do", 5), ("dy", 0, 4), ("back", 2), ("uz", 0, 3, 3), ("do", 3), ("dy", 1, 4),
    ("uz", 1, 3, 4), ("uz", 0, 2, 3), ("pre", 2), ("uz", 1, 2, 4), ("uz", 0, 1, 4), ("do", 4), ("back", 3),
    ("pre", 3), ("pre", 4), ("back", 4),
)
GELU_C = 0.7978845608028654
MESH = pl.DeviceIdType.MESH


def remote(src, dst, send, recv, where):
    return pltpu.make_async_remote_copy(
        src_ref=src, dst_ref=dst, send_sem=send, recv_sem=recv, device_id=where, device_id_type=MESH
    )


def row_halo(buf, send, recv, sx, act):
    down = remote(buf.at[:, 8:11, 8:24, :], buf.at[:, 0:3, 8:24, :], send.at[0], recv.at[0], {"sx": sx + 1})
    up = remote(buf.at[:, 3:6, 8:24, :], buf.at[:, 11:14, 8:24, :], send.at[1], recv.at[1], {"sx": sx - 1})
    if act == "start":

        @pl.when(sx < 3)
        def _():
            down.start()

        @pl.when(sx > 0)
        def _():
            up.start()

    else:

        @pl.when(sx < 3)
        def _():
            up.wait_recv()
            down.wait_send()

        @pl.when(sx > 0)
        def _():
            down.wait_recv()
            up.wait_send()


def zero_rows(buf, sx):
    @pl.when(sx == 0)
    def _():
        buf[:, 0:3, :, :] = jnp.zeros((NB, 3, PC, 128), jnp.float32)

    @pl.when(sx == 3)
    def _():
        buf[:, 11:14, :, :] = jnp.zeros((NB, 3, PC, 128), jnp.float32)


def pack_cols(buf, stage, sy):
    for side, first in ((0, 21), (1, 8)):

        @pl.when(sy == side)
        def _():
            @pl.loop(0, NB)
            def _(b):
                for c in range(3):
                    at = pl.multiple_of(b * 16, 16)
                    stage[c, pl.ds(at, 16), :] = buf[b, :, first + c, :].astype(jnp.bfloat16)


def unpack_cols(buf, stage, sy):
    for side, first, other in ((0, 24, 5), (1, 5, 24)):

        @pl.when(sy == side)
        def _():
            @pl.loop(0, NB)
            def _(b):
                for c in range(3):
                    at = pl.multiple_of(b * 16, 16)
                    buf[b, :, first + c, :] = stage[c, pl.ds(at, 16), :].astype(jnp.float32)
                    buf[b, :, other + c, :] = jnp.zeros((PR, 128), jnp.float32)


def lanes(b):
    return pl.ds(pl.multiple_of(b * 128, 128), 128)


def depthwise(buf, b, taps, start, flip):
    acc = start
    for j in range(KW):
        jj = 6 - j if flip else j
        shifted = buf[b, 0:14, 5 + jj : 21 + jj, :]
        for i in range(KW):
            ii = 6 - i if flip else i
            acc = acc + taps[i, j, lanes(b)].reshape(1, 1, 128) * shifted[ii : ii + ROWS]
    return acc


def kernel_grad(xbuf, gbuf, grads, b):
    g = gbuf[b, 3:11, 8:24, :]
    for j in range(KW):
        shifted = xbuf[b, 0:14, 5 + j : 21 + j, :]
        for i in range(KW):
            q = jnp.sum(g * shifted[i : i + ROWS], axis=0)
            grads[b * 7 + i, j, :] = jnp.sum(q, axis=0)


TOK = ROWS * COLS


def block_kernel(
    code, expo, cot, taps, dw_bias_in, ln_gain_in, ln_bias_in, w_up, b_up, w_down, b_down_in, layer_scale_in,
    bo, gi, gk, gg, gs,
    dw_bias, ln_gain, ln_bias, b_down, layer_scale, xp, gp, stage, landed, up, down, ln, dm, conv, rstd, pre, dact, act, dpre,
    mine_dln, send_dln, got_dln, mine_mlp, send_mlp, got_mlp,
    grads, got1, part, got2, fin, full,
    ls, vs, xus, xur, xds, xdr, a1s, a1r, azs, azr, bzs, bzr, bys, byr, bfs, bfr, ts, tr, dls, dlr, mls, mlr,
    hs, hr, cs, cr, s1, r1, s2, r2, s3, r3, s4, r4,
):
    sx, sy, f = lax.axis_index("sx"), lax.axis_index("sy"), lax.axis_index("fsdp")
    g = sx * 2 + sy
    half = lax.rem(sx, 2)
    other = {"sx": sx + 1 - 2 * half}
    z, y = f // 4, lax.rem(f, 4)
    f32, bf16 = jnp.float32, jnp.bfloat16

    def peer(k):
        p = lax.rem(g + k, 8)
        return p, {"sx": p // 2, "sy": lax.rem(p, 2)}

    x = sy * 2 + sx // 2
    odd_x = lax.rem(x, 2)
    missing = lambda buf: MISSING_UP if buf is up else MISSING_DOWN

    def x_peer(sign):
        to = lax.rem(x + sign + 4, 4)
        return {"sx": lax.rem(to, 2) * 2 + half, "sy": to // 2}

    def zz(d):
        return lax.rem(z + d + 8, 8)

    def yy(d):
        return lax.rem(y + d + 4, 4)

    def window(buf, start=0):
        return pl.ds(pl.multiple_of(start + odd_x * missing(buf), 128), CHANS - missing(buf))

    def shard(buf, dz, dy):
        return buf.at[pl.ds(pl.multiple_of((zz(dz) * 4 + yy(dy)) * 48, 16), 48), window(buf)]

    barrier = pltpu.get_barrier_semaphore()
    near = [{"fsdp": zz(1) * 4 + y}, {"fsdp": zz(-1) * 4 + y}]
    near += [{"fsdp": z * 4 + yy(k)} for k in (1, 2, 3)] + [peer(k)[1] for k in range(1, 8)]
    for where in near:
        pl.semaphore_signal(barrier, inc=1, device_id=where, device_id_type=MESH)

    own = [
        pltpu.make_async_copy(w_up.at[:, window(up, half * HID)], shard(up, 0, 0), ls.at[0]),
        pltpu.make_async_copy(w_down.at[:, window(down, half * HID)], shard(down, 0, 0), ls.at[1]),
    ]
    vectors = (
        (dw_bias_in, dw_bias), (ln_gain_in, ln_gain), (ln_bias_in, ln_bias), (b_down_in, b_down),
        (layer_scale_in, layer_scale),
    )
    rows_in = [pltpu.make_async_copy(src, dst.at[0], vs.at[n]) for n, (src, dst) in enumerate(vectors)]
    for copy in own + rows_in:
        copy.start()
    for copy in own:
        copy.wait()
    pl.semaphore_wait(barrier, len(near))

    sent = []

    def send(copy):
        copy.start()
        sent.append(copy)

    def up_y(k):
        return remote(shard(up, 0, 0), shard(up, 0, 0), a1s.at[k - 1], a1r.at[k - 1], {"fsdp": z * 4 + yy(k)})

    def up_y_got(k):
        return remote(shard(up, 0, -k), shard(up, 0, -k), a1s.at[k - 1], a1r.at[k - 1], {"fsdp": z * 4 + yy(k)})

    def up_z(way, k, s, got=False):
        sign = 1 - 2 * way
        block = shard(up, -sign * (s if got else s - 1), -k)
        at = way * 16 + k * 4 + s - 1
        return remote(block, block, azs.at[at], azr.at[at], {"fsdp": zz(sign) * 4 + y})

    def down_z(way, s, got=False):
        sign = 1 - 2 * way
        block = shard(down, -sign * (s if got else s - 1), 0)
        at = way * 4 + s - 1
        return remote(block, block, bzs.at[at], bzr.at[at], {"fsdp": zz(sign) * 4 + y})

    def down_y(way, d, got=False):
        sign = 1 - 2 * way
        block = shard(down, d, -sign if got else 0)
        at = way * 8 + d
        return remote(block, block, bys.at[at], byr.at[at], {"fsdp": z * 4 + yy(sign)})

    def down_on(d, got=False):
        sign = 1 - 2 * (d % 2)
        block = shard(down, d, 2 if got else -sign)
        return remote(block, block, bfs.at[d], bfr.at[d], {"fsdp": z * 4 + yy(sign)})

    def x_send(buf, d, dy, got=False):
        sends, recvs = (xus, xur) if buf is up else (xds, xdr)
        at = d % 8 * 4 + dy % 4
        rows = pl.ds(pl.multiple_of((zz(d) * 4 + yy(dy)) * 48, 16), 48)
        place = (1 - odd_x if got else odd_x) * (CHANS - missing(buf))
        block = buf.at[rows, pl.ds(pl.multiple_of(place, 128), missing(buf))]
        return remote(block, block, sends.at[at], recvs.at[at], x_peer(1 - 2 * ((d + dy) % 2)))

    def x_arrived(buf, step):
        for d in sorted({-step % 8, step}):
            for dy in (0, 1, -1, 2):
                x_send(buf, d, dy, True).wait_recv()

    def handle(kind, way, k=0, s=0):
        if kind == "uy":
            up_y_got(way).wait_recv()
            for to in (0, 1):
                send(up_z(to, way, 1))
            send(x_send(up, 0, -way))
        elif kind == "uz":
            up_z(way, k, s, True).wait_recv()
            if s < (4 if way == k // 2 else 3):
                send(up_z(way, k, s + 1))
            send(x_send(up, s if way else -s, -k))
        elif kind == "dz":
            down_z(way, k, True).wait_recv()
            if k < 4 - way:
                send(down_z(way, k + 1))
            d = k if way else 8 - k
            send(down_y(0, d))
            send(down_y(1, d))
            send(x_send(down, d, 0))
        elif kind == "dy":
            down_y(way, k, True).wait_recv()
            if k % 2 == way:
                send(down_on(k))
            send(x_send(down, k, 1 if way else -1))
        else:
            down_on(way, True).wait_recv()
            send(x_send(down, way, 2))

    send(up_y(1))
    send(up_y(3))
    for way in (0, 1):
        send(up_z(way, 0, 1))
        send(down_z(way, 1))
    send(up_y(2))
    for way in (0, 1):
        send(down_y(way, 0))
    send(x_send(up, 0, 0))
    send(x_send(down, 0, 0))

    factor = jnp.left_shift(1, expo[...] + 2).astype(f32) * 0.25
    for b in range(NB):
        at = slice(b * 128, (b + 1) * 128)
        scaled = code[:, :, at].astype(f32) * factor[:, :, b : b + 1]
        xp[b, 3:11, 8:24, :] = scaled
    zero_rows(xp, sx)
    row_halo(xp, hs.at[0], hr.at[0], sx, "start")

    def tokens(buf, at):
        return remote(buf.at[0:TOK], buf.at[TOK : 2 * TOK], ts.at[at], tr.at[at], other)

    def forward_conv(b):
        start = jnp.broadcast_to(dw_bias[:, lanes(b)].reshape(1, 1, 128), (ROWS, COLS, 128))
        conv[b] = depthwise(xp, b, taps, start, False).reshape(TOK, 128)

    xcol = remote(stage.at[0], landed.at[0], cs.at[0], cr.at[0], {"sy": 1 - sy})

    def tokens_task():
        for copy in rows_in:
            copy.wait()

        @pl.loop(0, NB)
        def _(b):
            ct = cot[:, :, lanes(b)].astype(f32).reshape(TOK, 128)
            dm[0:TOK, lanes(b)] = (layer_scale[:, lanes(b)] * ct).astype(bf16)

        send(tokens(dm, 0))
        zero_rows(gp, sx)
        grads[84:88] = jnp.zeros((4, 8, 128), f32)

    def xcols_task():
        row_halo(xp, hs.at[0], hr.at[0], sx, "wait")
        pack_cols(xp, stage.at[0], sy)
        xcol.start()

    def unpack_task():
        xcol.wait()
        unpack_cols(xp, landed.at[0], sy)

    def norm_task():
        def over_channels(term):
            total = lax.fori_loop(0, NB, lambda b, t: t + term(b), jnp.zeros((TOK, 128), f32))
            return jnp.sum(total, axis=1, keepdims=True) / CHANS

        mu = over_channels(lambda b: conv[b])
        var = over_channels(lambda b: (conv[b] - mu) * (conv[b] - mu))
        rstd[...] = jnp.broadcast_to(lax.rsqrt(var + 1e-6), (TOK, 128))

        @pl.loop(0, NB)
        def _(b):
            normed = (conv[b] - mu) * rstd[...]
            conv[b] = normed
            ln[0:TOK, lanes(b)] = (normed * ln_gain[:, lanes(b)] + ln_bias[:, lanes(b)]).astype(bf16)

        send(tokens(ln, 1))

    odd = lax.rem(z, 2)

    def tile(n):
        return pl.ds(pl.multiple_of(n * 256, 256), 256)

    def add_pre(s):
        base = (-odd, -2 + 3 * odd, 2 - 5 * odd, 4 - odd)[s - 1]
        rows = pl.ds(pl.multiple_of(zz(base) * 192, 384), 384)

        @pl.loop(0, 6)
        def _(n):
            term = jnp.dot(ln[:, rows], up[rows, tile(n)], preferred_element_type=f32)
            if s == 1:
                start = pl.multiple_of(half * HID + n * 256, 256)
                pre[:, tile(n)] = term + b_up[:, pl.ds(start, 256)]
            else:
                pre[:, tile(n)] = pre[:, tile(n)] + term

    def add_dact(s):
        base = (-odd, -2 + 3 * odd, 2 - 5 * odd, 4 - odd)[s - 1]
        rows = pl.ds(pl.multiple_of(zz(base) * 192, 384), 384)

        @pl.loop(0, 6)
        def _(n):
            term = jnp.dot(dm[:, rows], down[rows, tile(n)], preferred_element_type=f32)
            dact[:, tile(n)] = term if s == 1 else dact[:, tile(n)] + term

    for name, *rest in ORDER:
        if name == "tokens":
            tokens_task()
        elif name == "xcols":
            xcols_task()
        elif name == "unpack":
            unpack_task()
        elif name == "conv":
            pl.loop(rest[0], rest[0] + 3)(forward_conv)
        elif name == "norm":
            norm_task()
        elif name == "pre":
            if rest[0] == 1:
                tokens(ln, 1).wait_recv()
                x_arrived(up, 0)
            x_arrived(up, rest[0])
            add_pre(rest[0])
        elif name == "back":
            if rest[0] == 1:
                tokens(dm, 0).wait_recv()
                x_arrived(down, 0)
            x_arrived(down, rest[0])
            add_dact(rest[0])
        else:
            handle(name, *rest)

    @pl.loop(0, 12)
    def _(n):
        v = pre[:, lanes(n)]
        v2 = v * v
        t = jnp.tanh(GELU_C * v * (1.0 + 0.044715 * v2))
        cdf = 0.5 * (1.0 + t)
        act[:, lanes(n)] = (v * cdf).astype(bf16)
        slope = cdf + 0.5 * v * (1.0 - t * t) * (GELU_C * (1.0 + 3 * 0.044715 * v2))
        dpre[:, lanes(n)] = (dact[:, lanes(n)] * slope).astype(bf16)

    moved_dln = (send_dln, got_dln, dls, dlr)
    moved_mlp = (send_mlp, got_mlp, mls, mlr)

    def arrived(moved, n):
        src, dst, sends, recvs = moved
        return remote(src.at[:, tile(n)], dst.at[:, tile(n)], sends.at[n], recvs.at[n], other)

    def down_projection(lhs, weights, mine, moved):
        @pl.loop(0, 6)
        def _(n):
            out = lax.dot_general(
                lhs[...], weights[tile(n), :], (((1,), (1,)), ((), ())), preferred_element_type=f32
            )
            mine[:, tile(n)] = out[0:TOK]
            moved[0][:, tile(n)] = out[TOK : 2 * TOK]
            arrived(moved, n).start()

    down_projection(dpre, up, mine_dln, moved_dln)
    down_projection(act, down, mine_mlp, moved_mlp)

    def back_sums(b, sums):
        @pl.when(lax.rem(b, 2) == 0)
        def _():
            arrived(moved_dln, b // 2).wait_recv()

        d_ln = mine_dln[:, lanes(b)] + got_dln[:, lanes(b)]
        grads[b * 7, 7, :] = jnp.sum(d_ln * conv[b], axis=0)
        d_norm = d_ln * ln_gain[:, lanes(b)]
        mine_dln[:, lanes(b)] = d_norm
        return sums[0] + d_norm, sums[1] + d_norm * conv[b]

    zeros = jnp.zeros((TOK, 128), f32)
    sum_d, sum_dn = lax.fori_loop(0, NB, back_sums, (zeros, zeros))
    mean_d = jnp.sum(sum_d, axis=1, keepdims=True) / CHANS
    mean_dn = jnp.sum(sum_dn, axis=1, keepdims=True) / CHANS

    @pl.loop(0, NB)
    def _(b):
        d_conv = rstd[...] * (mine_dln[:, lanes(b)] - mean_d - conv[b] * mean_dn)
        gp[b, 3:11, 8:24, :] = d_conv.reshape(ROWS, COLS, 128)

    row_halo(gp, hs.at[1], hr.at[1], sx, "start")

    @pl.loop(0, 8)
    def _(b):
        kernel_grad(xp, gp, grads, b)

    row_halo(gp, hs.at[1], hr.at[1], sx, "wait")
    pack_cols(gp, stage.at[1], sy)
    col = remote(stage.at[1], landed.at[1], cs.at[1], cr.at[1], {"sy": 1 - sy})
    col.start()

    @pl.loop(0, NB)
    def _(b):
        @pl.when(lax.rem(b, 2) == 0)
        def _():
            arrived(moved_mlp, b // 2).wait_recv()

        mlp = (mine_mlp[:, lanes(b)] + got_mlp[:, lanes(b)]) + b_down[:, lanes(b)]
        ct = cot[:, :, lanes(b)].astype(jnp.float32).reshape(TOK, 128)
        grads[b * 7 + 1, 7, :] = jnp.sum(ct * mlp, axis=0)
        scaled = xp[b, 3:11, 8:24, :].reshape(TOK, 128)
        bo[:, lanes(b)] = (scaled + layer_scale[:, lanes(b)] * mlp).astype(jnp.bfloat16)
        for i in range(2, 7):
            grads[b * 7 + i, 7, :] = jnp.zeros((128,), jnp.float32)

    @pl.loop(8, NB)
    def _(b):
        kernel_grad(xp, gp, grads, b)

    first = []
    for k in range(1, 8):
        p, where = peer(k)
        first.append(remote(grads.at[pl.ds(p * PIECE, PIECE)], got1.at[k - 1], s1.at[k - 1], r1.at[k - 1], where))
        first[-1].start()

    col.wait()
    unpack_cols(gp, landed.at[1], sy)

    def out_conv(b):
        gi[:, :, lanes(b)] = depthwise(
            gp, b, taps, cot[:, :, lanes(b)].astype(jnp.float32), True
        ).astype(jnp.bfloat16)

    pl.loop(0, 4)(out_conv)

    total = grads[pl.ds(g * PIECE, PIECE)]
    for k in range(7):
        first[k].wait_recv()
        total = total + got1[k]
    part[...] = total

    def to_owner(t):
        owner = t * 3
        slot = lax.rem(f - owner + 32, 32)
        return remote(part.at[t], got2.at[slot], s2.at[t], r2.at[slot], {"fsdp": owner})

    for t in range(PIECE):

        @pl.when(f != t * 3)
        def _():
            to_owner(t).start()

    pl.loop(4, 8)(out_conv)

    mine = f // 3
    owns = lax.rem(f, 3) == 0

    def spread(k):
        return remote(fin.at[mine], fin.at[mine], s3.at[k], r3.at[mine], {"fsdp": lax.rem(f + k, 32)})

    @pl.when(owns)
    def _():
        fin[mine] = part[mine]

        @pl.loop(1, 32)
        def _(k):
            remote(part.at[0], got2.at[k], s2.at[0], r2.at[k], {"fsdp": f}).wait_recv()
            fin[mine] = fin[mine] + got2[k]

        @pl.loop(1, 32)
        def _(k):
            spread(k).start()

    pl.loop(8, NB)(out_conv)

    for t in range(PIECE):

        @pl.when(f != t * 3)
        def _():
            remote(fin.at[t], fin.at[t], s3.at[0], r3.at[t], {"fsdp": t * 3}).wait_recv()

    last = []
    for k in range(1, 8):
        p, where = peer(k)
        last.append(remote(fin, full.at[pl.ds(g * PIECE, PIECE)], s4.at[k - 1], r4.at[k - 1], where))
        last[-1].start()
    full[pl.ds(g * PIECE, PIECE)] = fin[...]
    for k in range(7):
        last[k].wait_recv()
    for b in range(NB):
        at = slice(b * 128, (b + 1) * 128)
        for i in range(KW):
            gk[i, :, at] = full[b * 7 + i, 0:7, :]
        gg[at] = full[b * 7, 7, :]
        gs[at] = full[b * 7 + 1, 7, :]

    for k in range(7):
        first[k].wait_send()
        last[k].wait_send()
    for t in range(PIECE):

        @pl.when(f != t * 3)
        def _():
            to_owner(t).wait_send()

    @pl.when(owns)
    def _():
        @pl.loop(1, 32)
        def _(k):
            spread(k).wait_send()

    for n in range(6):
        arrived(moved_dln, n).wait_send()
        arrived(moved_mlp, n).wait_send()
    for copy in sent:
        copy.wait_send()


def on_device(
    x_code, x_exp, dw_kernel, dw_bias, ln_gain, ln_bias, w_up, b_up, w_down, b_down, layer_scale, cotangent
):
    vmem = pl.BlockSpec(memory_space=pltpu.VMEM)
    anywhere = pl.BlockSpec(memory_space=pl.ANY)
    dma = pltpu.SemaphoreType.DMA
    f32, bf16 = jnp.float32, jnp.bfloat16
    row = lambda v: v.reshape(1, -1)
    tok_f32 = pltpu.VMEM((TOK, CHANS), f32)
    pair_f32, pair_bf16 = pltpu.VMEM((2 * TOK, HID), f32), pltpu.VMEM((2 * TOK, HID), bf16)
    weight = pltpu.VMEM((CHANS, HID), bf16)
    padded = pltpu.VMEM((NB, PR, PC, 128), f32)
    staged = pltpu.VMEM((2, 3, NB * 16, 128), bf16)
    block_out, grad_input, grad_kernel, grad_gain, grad_scale = pl.pallas_call(
        block_kernel,
        out_shape=(
            jax.ShapeDtypeStruct((TOK, CHANS), bf16),
            jax.ShapeDtypeStruct((ROWS, COLS, CHANS), bf16),
            jax.ShapeDtypeStruct((KW, KW, CHANS), f32),
            jax.ShapeDtypeStruct((CHANS,), f32),
            jax.ShapeDtypeStruct((CHANS,), f32),
        ),
        in_specs=[vmem] * 4 + [anywhere] * 4 + [vmem] + [anywhere] * 3,
        out_specs=(vmem,) * 5,
        scratch_shapes=[
            *[pltpu.VMEM((1, CHANS), f32)] * 5, padded, padded, staged, staged, weight, weight, pair_bf16, pair_bf16,
            pltpu.VMEM((NB, TOK, 128), f32), pltpu.VMEM((TOK, 128), f32),
            pair_f32, pair_f32, pair_bf16, pair_bf16,
            tok_f32, tok_f32, tok_f32, tok_f32, tok_f32, tok_f32,
            pltpu.VMEM((88, 8, 128), f32),
            pltpu.VMEM((7, PIECE, 8, 128), f32),
            pltpu.VMEM((PIECE, 8, 128), f32),
            pltpu.VMEM((32, 8, 128), f32),
            pltpu.VMEM((PIECE, 8, 128), f32),
            pltpu.VMEM((88, 8, 128), f32),
            dma((2,)), dma((5,)), dma((32,)), dma((32,)), dma((32,)), dma((32,)),
            dma((3,)), dma((3,)), dma((32,)), dma((32,)), dma((8,)), dma((8,)),
            dma((16,)), dma((16,)), dma((8,)), dma((8,)), dma((2,)), dma((2,)),
            dma((6,)), dma((6,)), dma((6,)), dma((6,)),
            dma((2, 2)), dma((2, 2)), dma((2,)), dma((2,)),
            dma((7,)), dma((7,)), dma((PIECE,)), dma((32,)),
            dma((32,)), dma((PIECE,)), dma((7,)), dma((7,)),
        ],
        compiler_params=pltpu.CompilerParams(
            collective_id=1, has_side_effects=True, vmem_limit_bytes=56 * 2**20
        ),
        name="block",
    )(
        x_code[0], x_exp[0], cotangent[0], dw_kernel, dw_bias, ln_gain, ln_bias,
        w_up, row(b_up), w_down.T, b_down, layer_scale,
    )
    return (
        block_out.reshape(1, ROWS, COLS, CHANS), grad_input[None], grad_kernel, grad_gain, grad_scale
    )


def solution(mesh):
    placed = (
        P("fsdp", "sx", "sy", None),
        P("fsdp", "sx", "sy", None),
        P(),
        P(),
        P(),
        P(),
        P("fsdp", None),
        P(),
        P(None, "fsdp"),
        P(),
        P(),
        P("fsdp", "sx", "sy", None),
    )
    return jax.shard_map(
        on_device,
        mesh=mesh,
        in_specs=placed,
        out_specs=(P("fsdp", "sx", "sy", None), P("fsdp", "sx", "sy", None), P(), P(), P()),
        check_vma=False,
    )
```

```python
import jax
import jax.numpy as jnp
from jax import lax
from jax.experimental import pallas as pl
from jax.experimental.pallas import tpu as pltpu
from jax.sharding import PartitionSpec as P

CG = 128
KW = 7
NB = 12
ROWS, COLS, CHANS = 8, 16, 1536
PR, PC = 16, 32
PIECE = 11
HID = 1536
MISSING_UP, MISSING_DOWN = 640, 512
ORDER = (
    ("uz", 0, 0, 1), ("uz", 1, 0, 1), ("uy", 1), ("uy", 3), ("uy", 2), ("tokens",), ("dz", 0, 1),
    ("dz", 1, 1), ("dy", 0, 0), ("dy", 1, 0), ("xcols",), ("uz", 0, 0, 2), ("uz", 1, 0, 2), ("dy", 0, 7),
    ("dy", 1, 7), ("uz", 0, 1, 1), ("uz", 1, 1, 1), ("uz", 0, 3, 1), ("uz", 1, 3, 1), ("dy", 0, 1),
    ("dy", 1, 1), ("do", 0), ("dz", 0, 2), ("dz", 1, 2), ("uz", 0, 2, 1), ("uz", 1, 2, 1), ("unpack",),
    ("conv", 0), ("do", 7), ("dy", 0, 6), ("uz", 0, 0, 3), ("uz", 1, 0, 3), ("conv", 3), ("do", 1),
    ("dy", 1, 6), ("dy", 0, 2), ("uz", 0, 1, 2), ("uz", 1, 1, 2), ("conv", 6), ("dz", 0, 3), ("dz", 1, 3),
    ("dy", 1, 2), ("uz", 0, 3, 2), ("uz", 1, 3, 2), ("conv", 9), ("do", 6), ("norm",), ("dy", 1, 5),
    ("uz", 0, 2, 2), ("uz", 1, 2, 2), ("do", 2), ("dy", 0, 5), ("dy", 1, 3), ("uz", 0, 0, 4),
    ("uz", 1, 1, 3), ("back", 1), ("dz", 0, 4), ("dy", 0, 3), ("uz", 0, 1, 3), ("uz", 1, 3, 3), ("pre", 1),
    ("uz", 1, 2, 3), ("do", 5), ("dy", 0, 4), ("back", 2), ("uz", 0, 3, 3), ("do", 3), ("dy", 1, 4),
    ("uz", 1, 3, 4), ("uz", 0, 2, 3), ("pre", 2), ("uz", 1, 2, 4), ("uz", 0, 1, 4), ("do", 4), ("back", 3),
    ("pre", 3), ("pre", 4), ("back", 4),
)
GELU_C = 0.7978845608028654
MESH = pl.DeviceIdType.MESH


def remote(src, dst, send, recv, where):
    return pltpu.make_async_remote_copy(
        src_ref=src, dst_ref=dst, send_sem=send, recv_sem=recv, device_id=where, device_id_type=MESH
    )


def row_halo(buf, send, recv, sx, act):
    down = remote(buf.at[:, 8:11, 8:24, :], buf.at[:, 0:3, 8:24, :], send.at[0], recv.at[0], {"sx": sx + 1})
    up = remote(buf.at[:, 3:6, 8:24, :], buf.at[:, 11:14, 8:24, :], send.at[1], recv.at[1], {"sx": sx - 1})
    if act == "start":

        @pl.when(sx < 3)
        def _():
            down.start()

        @pl.when(sx > 0)
        def _():
            up.start()

    else:

        @pl.when(sx < 3)
        def _():
            up.wait_recv()
            down.wait_send()

        @pl.when(sx > 0)
        def _():
            down.wait_recv()
            up.wait_send()


def zero_rows(buf, sx):
    @pl.when(sx == 0)
    def _():
        buf[:, 0:3, :, :] = jnp.zeros((NB, 3, PC, 128), jnp.float32)

    @pl.when(sx == 3)
    def _():
        buf[:, 11:14, :, :] = jnp.zeros((NB, 3, PC, 128), jnp.float32)


def pack_cols(buf, stage, sy):
    for side, first in ((0, 21), (1, 8)):

        @pl.when(sy == side)
        def _():
            @pl.loop(0, NB)
            def _(b):
                for c in range(3):
                    at = pl.multiple_of(b * 16, 16)
                    stage[c, pl.ds(at, 16), :] = buf[b, :, first + c, :].astype(jnp.bfloat16)


def unpack_cols(buf, stage, sy):
    for side, first, other in ((0, 24, 5), (1, 5, 24)):

        @pl.when(sy == side)
        def _():
            @pl.loop(0, NB)
            def _(b):
                for c in range(3):
                    at = pl.multiple_of(b * 16, 16)
                    buf[b, :, first + c, :] = stage[c, pl.ds(at, 16), :].astype(jnp.float32)
                    buf[b, :, other + c, :] = jnp.zeros((PR, 128), jnp.float32)


def lanes(b):
    return pl.ds(pl.multiple_of(b * 128, 128), 128)


def depthwise(buf, b, taps, start, flip):
    acc = start
    for j in range(KW):
        jj = 6 - j if flip else j
        shifted = buf[b, 0:14, 5 + jj : 21 + jj, :]
        for i in range(KW):
            ii = 6 - i if flip else i
            acc = acc + taps[i, j, lanes(b)].reshape(1, 1, 128) * shifted[ii : ii + ROWS]
    return acc


def kernel_grad(xbuf, gbuf, grads, b):
    g = gbuf[b, 3:11, 8:24, :]
    for j in range(KW):
        shifted = xbuf[b, 0:14, 5 + j : 21 + j, :]
        for i in range(KW):
            q = jnp.sum(g * shifted[i : i + ROWS], axis=0)
            grads[b * 7 + i, j, :] = jnp.sum(q, axis=0)


TOK = ROWS * COLS


def block_kernel(
    code, expo, cot, taps, dw_bias_in, ln_gain_in, ln_bias_in, w_up, b_up, w_down, b_down_in, layer_scale_in,
    bo, gi, gk, gg, gs,
    dw_bias, ln_gain, ln_bias, b_down, layer_scale, xp, gp, stage, landed, up, down, ln, dm, conv, rstd, pre, dact, act, dpre,
    mine_dln, send_dln, got_dln, mine_mlp, send_mlp, got_mlp,
    grads, got1, part, got2, fin, full,
    ls, vs, xus, xur, xds, xdr, a1s, a1r, azs, azr, bzs, bzr, bys, byr, bfs, bfr, ts, tr, dls, dlr, mls, mlr,
    hs, hr, cs, cr, s1, r1, s2, r2, s3, r3, s4, r4,
):
    sx, sy, f = lax.axis_index("sx"), lax.axis_index("sy"), lax.axis_index("fsdp")
    g = sx * 2 + sy
    half = lax.rem(sx, 2)
    other = {"sx": sx + 1 - 2 * half}
    z, y = f // 4, lax.rem(f, 4)
    f32, bf16 = jnp.float32, jnp.bfloat16

    def peer(k):
        p = lax.rem(g + k, 8)
        return p, {"sx": p // 2, "sy": lax.rem(p, 2)}

    x = sy * 2 + sx // 2
    odd_x = lax.rem(x, 2)
    missing = lambda buf: MISSING_UP if buf is up else MISSING_DOWN

    def x_peer(sign):
        to = lax.rem(x + sign + 4, 4)
        return {"sx": lax.rem(to, 2) * 2 + half, "sy": to // 2}

    def zz(d):
        return lax.rem(z + d + 8, 8)

    def yy(d):
        return lax.rem(y + d + 4, 4)

    def window(buf, start=0):
        return pl.ds(pl.multiple_of(start + odd_x * missing(buf), 128), CHANS - missing(buf))

    def shard(buf, dz, dy):
        return buf.at[pl.ds(pl.multiple_of((zz(dz) * 4 + yy(dy)) * 48, 16), 48), window(buf)]

    barrier = pltpu.get_barrier_semaphore()
    near = [{"fsdp": zz(1) * 4 + y}, {"fsdp": zz(-1) * 4 + y}]
    near += [{"fsdp": z * 4 + yy(k)} for k in (1, 2, 3)] + [peer(k)[1] for k in range(1, 8)]
    for where in near:
        pl.semaphore_signal(barrier, inc=1, device_id=where, device_id_type=MESH)

    own = [
        pltpu.make_async_copy(w_up.at[:, window(up, half * HID)], shard(up, 0, 0), ls.at[0]),
        pltpu.make_async_copy(w_down.at[:, window(down, half * HID)], shard(down, 0, 0), ls.at[1]),
    ]
    vectors = (
        (dw_bias_in, dw_bias), (ln_gain_in, ln_gain), (ln_bias_in, ln_bias), (b_down_in, b_down),
        (layer_scale_in, layer_scale),
    )
    rows_in = [pltpu.make_async_copy(src, dst.at[0], vs.at[n]) for n, (src, dst) in enumerate(vectors)]
    for copy in own + rows_in:
        copy.start()
    for copy in own:
        copy.wait()
    pl.semaphore_wait(barrier, len(near))

    sent = []

    def send(copy):
        copy.start()
        sent.append(copy)

    def up_y(k):
        return remote(shard(up, 0, 0), shard(up, 0, 0), a1s.at[k - 1], a1r.at[k - 1], {"fsdp": z * 4 + yy(k)})

    def up_y_got(k):
        return remote(shard(up, 0, -k), shard(up, 0, -k), a1s.at[k - 1], a1r.at[k - 1], {"fsdp": z * 4 + yy(k)})

    def up_z(way, k, s, got=False):
        sign = 1 - 2 * way
        block = shard(up, -sign * (s if got else s - 1), -k)
        at = way * 16 + k * 4 + s - 1
        return remote(block, block, azs.at[at], azr.at[at], {"fsdp": zz(sign) * 4 + y})

    def down_z(way, s, got=False):
        sign = 1 - 2 * way
        block = shard(down, -sign * (s if got else s - 1), 0)
        at = way * 4 + s - 1
        return remote(block, block, bzs.at[at], bzr.at[at], {"fsdp": zz(sign) * 4 + y})

    def down_y(way, d, got=False):
        sign = 1 - 2 * way
        block = shard(down, d, -sign if got else 0)
        at = way * 8 + d
        return remote(block, block, bys.at[at], byr.at[at], {"fsdp": z * 4 + yy(sign)})

    def down_on(d, got=False):
        sign = 1 - 2 * (d % 2)
        block = shard(down, d, 2 if got else -sign)
        return remote(block, block, bfs.at[d], bfr.at[d], {"fsdp": z * 4 + yy(sign)})

    def x_send(buf, d, dy, got=False):
        sends, recvs = (xus, xur) if buf is up else (xds, xdr)
        at = d % 8 * 4 + dy % 4
        rows = pl.ds(pl.multiple_of((zz(d) * 4 + yy(dy)) * 48, 16), 48)
        place = (1 - odd_x if got else odd_x) * (CHANS - missing(buf))
        block = buf.at[rows, pl.ds(pl.multiple_of(place, 128), missing(buf))]
        return remote(block, block, sends.at[at], recvs.at[at], x_peer(1 - 2 * ((d + dy) % 2)))

    def x_arrived(buf, step):
        for d in sorted({-step % 8, step}):
            for dy in (0, 1, -1, 2):
                x_send(buf, d, dy, True).wait_recv()

    def handle(kind, way, k=0, s=0):
        if kind == "uy":
            up_y_got(way).wait_recv()
            for to in (0, 1):
                send(up_z(to, way, 1))
            send(x_send(up, 0, -way))
        elif kind == "uz":
            up_z(way, k, s, True).wait_recv()
            if s < (4 if way == k // 2 else 3):
                send(up_z(way, k, s + 1))
            send(x_send(up, s if way else -s, -k))
        elif kind == "dz":
            down_z(way, k, True).wait_recv()
            if k < 4 - way:
                send(down_z(way, k + 1))
            d = k if way else 8 - k
            send(down_y(0, d))
            send(down_y(1, d))
            send(x_send(down, d, 0))
        elif kind == "dy":
            down_y(way, k, True).wait_recv()
            if k % 2 == way:
                send(down_on(k))
            send(x_send(down, k, 1 if way else -1))
        else:
            down_on(way, True).wait_recv()
            send(x_send(down, way, 2))

    send(up_y(1))
    send(up_y(3))
    for way in (0, 1):
        send(up_z(way, 0, 1))
        send(down_z(way, 1))
    send(up_y(2))
    for way in (0, 1):
        send(down_y(way, 0))
    send(x_send(up, 0, 0))
    send(x_send(down, 0, 0))

    for b in range(NB):
        at = slice(b * 128, (b + 1) * 128)
        factor = jnp.left_shift(1, expo[b] + 2).astype(f32) * 0.25
        scaled = code[:, :, at].astype(f32) * factor[:, :, None]
        xp[b, 3:11, 8:24, :] = scaled
    zero_rows(xp, sx)
    row_halo(xp, hs.at[0], hr.at[0], sx, "start")

    def tokens(buf, at):
        return remote(buf.at[0:TOK], buf.at[TOK : 2 * TOK], ts.at[at], tr.at[at], other)

    def forward_conv(b):
        start = jnp.broadcast_to(dw_bias[:, lanes(b)].reshape(1, 1, 128), (ROWS, COLS, 128))
        conv[b] = depthwise(xp, b, taps, start, False).reshape(TOK, 128)

    xcol = remote(stage.at[0], landed.at[0], cs.at[0], cr.at[0], {"sy": 1 - sy})

    def tokens_task():
        for copy in rows_in:
            copy.wait()

        @pl.loop(0, NB)
        def _(b):
            ct = cot[:, :, lanes(b)].astype(f32).reshape(TOK, 128)
            dm[0:TOK, lanes(b)] = (layer_scale[:, lanes(b)] * ct).astype(bf16)

        send(tokens(dm, 0))
        zero_rows(gp, sx)
        grads[84:88] = jnp.zeros((4, 8, 128), f32)

    def xcols_task():
        row_halo(xp, hs.at[0], hr.at[0], sx, "wait")
        pack_cols(xp, stage.at[0], sy)
        xcol.start()

    def unpack_task():
        xcol.wait()
        unpack_cols(xp, landed.at[0], sy)

    def norm_task():
        def over_channels(term):
            total = lax.fori_loop(0, NB, lambda b, t: t + term(b), jnp.zeros((TOK, 128), f32))
            return jnp.sum(total, axis=1, keepdims=True) / CHANS

        mu = over_channels(lambda b: conv[b])
        var = over_channels(lambda b: (conv[b] - mu) * (conv[b] - mu))
        rstd[...] = jnp.broadcast_to(lax.rsqrt(var + 1e-6), (TOK, 128))

        @pl.loop(0, NB)
        def _(b):
            normed = (conv[b] - mu) * rstd[...]
            conv[b] = normed
            ln[0:TOK, lanes(b)] = (normed * ln_gain[:, lanes(b)] + ln_bias[:, lanes(b)]).astype(bf16)

        send(tokens(ln, 1))

    odd = lax.rem(z, 2)

    def tile(n):
        return pl.ds(pl.multiple_of(n * 256, 256), 256)

    def add_pre(s):
        base = (-odd, -2 + 3 * odd, 2 - 5 * odd, 4 - odd)[s - 1]
        rows = pl.ds(pl.multiple_of(zz(base) * 192, 384), 384)

        @pl.loop(0, 6)
        def _(n):
            term = jnp.dot(ln[:, rows], up[rows, tile(n)], preferred_element_type=f32)
            if s == 1:
                start = pl.multiple_of(half * HID + n * 256, 256)
                pre[:, tile(n)] = term + b_up[:, pl.ds(start, 256)]
            else:
                pre[:, tile(n)] = pre[:, tile(n)] + term

    def add_dact(s):
        base = (-odd, -2 + 3 * odd, 2 - 5 * odd, 4 - odd)[s - 1]
        rows = pl.ds(pl.multiple_of(zz(base) * 192, 384), 384)

        @pl.loop(0, 6)
        def _(n):
            term = jnp.dot(dm[:, rows], down[rows, tile(n)], preferred_element_type=f32)
            dact[:, tile(n)] = term if s == 1 else dact[:, tile(n)] + term

    for name, *rest in ORDER:
        if name == "tokens":
            tokens_task()
        elif name == "xcols":
            xcols_task()
        elif name == "unpack":
            unpack_task()
        elif name == "conv":
            pl.loop(rest[0], rest[0] + 3)(forward_conv)
        elif name == "norm":
            norm_task()
        elif name == "pre":
            if rest[0] == 1:
                tokens(ln, 1).wait_recv()
                x_arrived(up, 0)
            x_arrived(up, rest[0])
            add_pre(rest[0])
        elif name == "back":
            if rest[0] == 1:
                tokens(dm, 0).wait_recv()
                x_arrived(down, 0)
            x_arrived(down, rest[0])
            add_dact(rest[0])
        else:
            handle(name, *rest)

    @pl.loop(0, 12)
    def _(n):
        v = pre[:, lanes(n)]
        v2 = v * v
        t = jnp.tanh(GELU_C * v * (1.0 + 0.044715 * v2))
        cdf = 0.5 * (1.0 + t)
        act[:, lanes(n)] = (v * cdf).astype(bf16)
        slope = cdf + 0.5 * v * (1.0 - t * t) * (GELU_C * (1.0 + 3 * 0.044715 * v2))
        dpre[:, lanes(n)] = (dact[:, lanes(n)] * slope).astype(bf16)

    moved_dln = (send_dln, got_dln, dls, dlr)
    moved_mlp = (send_mlp, got_mlp, mls, mlr)

    def wide(n):
        return pl.ds(pl.multiple_of(n * 512, 512), 512)

    def arrived(moved, n):
        src, dst, sends, recvs = moved
        return remote(src.at[:, wide(n)], dst.at[:, wide(n)], sends.at[n], recvs.at[n], other)

    def down_projection(lhs, weights, mine, moved):
        @pl.loop(0, 3)
        def _(n):
            out = lax.dot_general(
                lhs[...], weights[wide(n), :], (((1,), (1,)), ((), ())), preferred_element_type=f32
            )
            mine[:, wide(n)] = out[0:TOK]
            moved[0][:, wide(n)] = out[TOK : 2 * TOK]
            arrived(moved, n).start()

    down_projection(dpre, up, mine_dln, moved_dln)
    down_projection(act, down, mine_mlp, moved_mlp)

    def back_sums(b, sums):
        @pl.when(lax.rem(b, 4) == 0)
        def _():
            arrived(moved_dln, b // 4).wait_recv()

        d_ln = mine_dln[:, lanes(b)] + got_dln[:, lanes(b)]
        grads[b * 7, 7, :] = jnp.sum(d_ln * conv[b], axis=0)
        d_norm = d_ln * ln_gain[:, lanes(b)]
        mine_dln[:, lanes(b)] = d_norm
        return sums[0] + d_norm, sums[1] + d_norm * conv[b]

    zeros = jnp.zeros((TOK, 128), f32)
    sum_d, sum_dn = lax.fori_loop(0, NB, back_sums, (zeros, zeros))
    mean_d = jnp.sum(sum_d, axis=1, keepdims=True) / CHANS
    mean_dn = jnp.sum(sum_dn, axis=1, keepdims=True) / CHANS

    @pl.loop(0, NB)
    def _(b):
        d_conv = rstd[...] * (mine_dln[:, lanes(b)] - mean_d - conv[b] * mean_dn)
        gp[b, 3:11, 8:24, :] = d_conv.reshape(ROWS, COLS, 128)

    row_halo(gp, hs.at[1], hr.at[1], sx, "start")

    @pl.loop(0, 8)
    def _(b):
        kernel_grad(xp, gp, grads, b)

    row_halo(gp, hs.at[1], hr.at[1], sx, "wait")
    pack_cols(gp, stage.at[1], sy)
    col = remote(stage.at[1], landed.at[1], cs.at[1], cr.at[1], {"sy": 1 - sy})
    col.start()

    @pl.loop(0, NB)
    def _(b):
        @pl.when(lax.rem(b, 4) == 0)
        def _():
            arrived(moved_mlp, b // 4).wait_recv()

        mlp = (mine_mlp[:, lanes(b)] + got_mlp[:, lanes(b)]) + b_down[:, lanes(b)]
        ct = cot[:, :, lanes(b)].astype(jnp.float32).reshape(TOK, 128)
        grads[b * 7 + 1, 7, :] = jnp.sum(ct * mlp, axis=0)
        scaled = xp[b, 3:11, 8:24, :].reshape(TOK, 128)
        bo[:, lanes(b)] = (scaled + layer_scale[:, lanes(b)] * mlp).astype(jnp.bfloat16)
        for i in range(2, 7):
            grads[b * 7 + i, 7, :] = jnp.zeros((128,), jnp.float32)

    @pl.loop(8, NB)
    def _(b):
        kernel_grad(xp, gp, grads, b)

    first = []
    for k in range(1, 8):
        p, where = peer(k)
        first.append(remote(grads.at[pl.ds(p * PIECE, PIECE)], got1.at[k - 1], s1.at[k - 1], r1.at[k - 1], where))
        first[-1].start()

    col.wait()
    unpack_cols(gp, landed.at[1], sy)

    def out_conv(b):
        gi[:, :, lanes(b)] = depthwise(
            gp, b, taps, cot[:, :, lanes(b)].astype(jnp.float32), True
        ).astype(jnp.bfloat16)

    pl.loop(0, 4)(out_conv)

    total = grads[pl.ds(g * PIECE, PIECE)]
    for k in range(7):
        first[k].wait_recv()
        total = total + got1[k]
    part[...] = total

    def to_owner(t):
        owner = t * 3
        slot = lax.rem(f - owner + 32, 32)
        return remote(part.at[t], got2.at[slot], s2.at[t], r2.at[slot], {"fsdp": owner})

    for t in range(PIECE):

        @pl.when(f != t * 3)
        def _():
            to_owner(t).start()

    pl.loop(4, 8)(out_conv)

    mine = f // 3
    owns = lax.rem(f, 3) == 0

    def spread(k):
        return remote(fin.at[mine], fin.at[mine], s3.at[k], r3.at[mine], {"fsdp": lax.rem(f + k, 32)})

    @pl.when(owns)
    def _():
        fin[mine] = part[mine]

        @pl.loop(1, 32)
        def _(k):
            remote(part.at[0], got2.at[k], s2.at[0], r2.at[k], {"fsdp": f}).wait_recv()
            fin[mine] = fin[mine] + got2[k]

        @pl.loop(1, 32)
        def _(k):
            spread(k).start()

    pl.loop(8, NB)(out_conv)

    for t in range(PIECE):

        @pl.when(f != t * 3)
        def _():
            remote(fin.at[t], fin.at[t], s3.at[0], r3.at[t], {"fsdp": t * 3}).wait_recv()

    last = []
    for k in range(1, 8):
        p, where = peer(k)
        last.append(remote(fin, full.at[pl.ds(g * PIECE, PIECE)], s4.at[k - 1], r4.at[k - 1], where))
        last[-1].start()
    full[pl.ds(g * PIECE, PIECE)] = fin[...]
    for k in range(7):
        last[k].wait_recv()
    for b in range(NB):
        at = slice(b * 128, (b + 1) * 128)
        for i in range(KW):
            gk[i, :, at] = full[b * 7 + i, 0:7, :]
        gg[at] = full[b * 7, 7, :]
        gs[at] = full[b * 7 + 1, 7, :]

    for k in range(7):
        first[k].wait_send()
        last[k].wait_send()
    for t in range(PIECE):

        @pl.when(f != t * 3)
        def _():
            to_owner(t).wait_send()

    @pl.when(owns)
    def _():
        @pl.loop(1, 32)
        def _(k):
            spread(k).wait_send()

    for n in range(3):
        arrived(moved_dln, n).wait_send()
        arrived(moved_mlp, n).wait_send()
    for copy in sent:
        copy.wait_send()


def on_device(
    x_code, x_exp, dw_kernel, dw_bias, ln_gain, ln_bias, w_up, b_up, w_down, b_down, layer_scale, cotangent
):
    vmem = pl.BlockSpec(memory_space=pltpu.VMEM)
    anywhere = pl.BlockSpec(memory_space=pl.ANY)
    dma = pltpu.SemaphoreType.DMA
    f32, bf16 = jnp.float32, jnp.bfloat16
    row = lambda v: v.reshape(1, -1)
    tok_f32 = pltpu.VMEM((TOK, CHANS), f32)
    pair_f32, pair_bf16 = pltpu.VMEM((2 * TOK, HID), f32), pltpu.VMEM((2 * TOK, HID), bf16)
    weight = pltpu.VMEM((CHANS, HID), bf16)
    padded = pltpu.VMEM((NB, PR, PC, 128), f32)
    staged = pltpu.VMEM((2, 3, NB * 16, 128), bf16)
    block_out, grad_input, grad_kernel, grad_gain, grad_scale = pl.pallas_call(
        block_kernel,
        out_shape=(
            jax.ShapeDtypeStruct((TOK, CHANS), bf16),
            jax.ShapeDtypeStruct((ROWS, COLS, CHANS), bf16),
            jax.ShapeDtypeStruct((KW, KW, CHANS), f32),
            jax.ShapeDtypeStruct((CHANS,), f32),
            jax.ShapeDtypeStruct((CHANS,), f32),
        ),
        in_specs=[vmem] * 4 + [anywhere] * 4 + [vmem] + [anywhere] * 3,
        out_specs=(vmem,) * 5,
        scratch_shapes=[
            *[pltpu.VMEM((1, CHANS), f32)] * 5, padded, padded, staged, staged, weight, weight, pair_bf16, pair_bf16,
            pltpu.VMEM((NB, TOK, 128), f32), pltpu.VMEM((TOK, 128), f32),
            pair_f32, pair_f32, pair_bf16, pair_bf16,
            tok_f32, tok_f32, tok_f32, tok_f32, tok_f32, tok_f32,
            pltpu.VMEM((88, 8, 128), f32),
            pltpu.VMEM((7, PIECE, 8, 128), f32),
            pltpu.VMEM((PIECE, 8, 128), f32),
            pltpu.VMEM((32, 8, 128), f32),
            pltpu.VMEM((PIECE, 8, 128), f32),
            pltpu.VMEM((88, 8, 128), f32),
            dma((2,)), dma((5,)), dma((32,)), dma((32,)), dma((32,)), dma((32,)),
            dma((3,)), dma((3,)), dma((32,)), dma((32,)), dma((8,)), dma((8,)),
            dma((16,)), dma((16,)), dma((8,)), dma((8,)), dma((2,)), dma((2,)),
            dma((6,)), dma((6,)), dma((6,)), dma((6,)),
            dma((2, 2)), dma((2, 2)), dma((2,)), dma((2,)),
            dma((7,)), dma((7,)), dma((PIECE,)), dma((32,)),
            dma((32,)), dma((PIECE,)), dma((7,)), dma((7,)),
        ],
        compiler_params=pltpu.CompilerParams(
            collective_id=1, has_side_effects=True, vmem_limit_bytes=56 * 2**20
        ),
        name="block",
    )(
        x_code[0], x_exp[0].transpose(2, 0, 1), cotangent[0], dw_kernel, dw_bias, ln_gain, ln_bias,
        w_up, row(b_up), w_down.T, b_down, layer_scale,
    )
    return (
        block_out.reshape(1, ROWS, COLS, CHANS), grad_input[None], grad_kernel, grad_gain, grad_scale
    )


def solution(mesh):
    placed = (
        P("fsdp", "sx", "sy", None),
        P("fsdp", "sx", "sy", None),
        P(),
        P(),
        P(),
        P(),
        P("fsdp", None),
        P(),
        P(None, "fsdp"),
        P(),
        P(),
        P("fsdp", "sx", "sy", None),
    )
    return jax.shard_map(
        on_device,
        mesh=mesh,
        in_specs=placed,
        out_specs=(P("fsdp", "sx", "sy", None), P("fsdp", "sx", "sy", None), P(), P(), P()),
        check_vma=False,
    )
```

```python
import jax
import jax.numpy as jnp
from jax import lax
from jax.experimental import pallas as pl
from jax.experimental.pallas import tpu as pltpu
from jax.sharding import PartitionSpec as P

CG = 128
KW = 7
NB = 12
ROWS, COLS, CHANS = 8, 16, 1536
PR, PC = 16, 32
PIECE = 11
HID = 1536
MISSING_UP, MISSING_DOWN = 640, 512
ORDER = (
    ("uz", 0, 0, 1), ("uz", 1, 0, 1), ("uy", 1), ("uy", 3), ("uy", 2), ("tokens",), ("dz", 0, 1),
    ("dz", 1, 1), ("dy", 0, 0), ("dy", 1, 0), ("xcols",), ("uz", 0, 0, 2), ("uz", 1, 0, 2), ("dy", 0, 7),
    ("dy", 1, 7), ("uz", 0, 1, 1), ("uz", 1, 1, 1), ("uz", 0, 3, 1), ("uz", 1, 3, 1), ("dy", 0, 1),
    ("dy", 1, 1), ("do", 0), ("dz", 0, 2), ("dz", 1, 2), ("uz", 0, 2, 1), ("uz", 1, 2, 1), ("unpack",),
    ("conv", 0), ("do", 7), ("dy", 0, 6), ("uz", 0, 0, 3), ("uz", 1, 0, 3), ("conv", 3), ("do", 1),
    ("dy", 1, 6), ("dy", 0, 2), ("uz", 0, 1, 2), ("uz", 1, 1, 2), ("conv", 6), ("dz", 0, 3), ("dz", 1, 3),
    ("dy", 1, 2), ("uz", 0, 3, 2), ("uz", 1, 3, 2), ("conv", 9), ("do", 6), ("norm",), ("dy", 1, 5),
    ("uz", 0, 2, 2), ("uz", 1, 2, 2), ("do", 2), ("dy", 0, 5), ("dy", 1, 3), ("uz", 0, 0, 4),
    ("uz", 1, 1, 3), ("back", 1), ("dz", 0, 4), ("dy", 0, 3), ("uz", 0, 1, 3), ("uz", 1, 3, 3), ("pre", 1),
    ("uz", 1, 2, 3), ("do", 5), ("dy", 0, 4), ("back", 2), ("uz", 0, 3, 3), ("do", 3), ("dy", 1, 4),
    ("uz", 1, 3, 4), ("uz", 0, 2, 3), ("pre", 2), ("uz", 1, 2, 4), ("uz", 0, 1, 4), ("do", 4), ("back", 3),
    ("pre", 3), ("pre", 4), ("back", 4),
)
GELU_C = 0.7978845608028654
MESH = pl.DeviceIdType.MESH


def remote(src, dst, send, recv, where):
    return pltpu.make_async_remote_copy(
        src_ref=src, dst_ref=dst, send_sem=send, recv_sem=recv, device_id=where, device_id_type=MESH
    )


def row_halo(buf, send, recv, sx, act):
    down = remote(buf.at[:, 8:11, 8:24, :], buf.at[:, 0:3, 8:24, :], send.at[0], recv.at[0], {"sx": sx + 1})
    up = remote(buf.at[:, 3:6, 8:24, :], buf.at[:, 11:14, 8:24, :], send.at[1], recv.at[1], {"sx": sx - 1})
    if act == "start":

        @pl.when(sx < 3)
        def _():
            down.start()

        @pl.when(sx > 0)
        def _():
            up.start()

    else:

        @pl.when(sx < 3)
        def _():
            up.wait_recv()
            down.wait_send()

        @pl.when(sx > 0)
        def _():
            down.wait_recv()
            up.wait_send()


def zero_rows(buf, sx):
    @pl.when(sx == 0)
    def _():
        buf[:, 0:3, :, :] = jnp.zeros((NB, 3, PC, 128), jnp.float32)

    @pl.when(sx == 3)
    def _():
        buf[:, 11:14, :, :] = jnp.zeros((NB, 3, PC, 128), jnp.float32)


def pack_cols(buf, stage, sy):
    for side, first in ((0, 21), (1, 8)):

        @pl.when(sy == side)
        def _():
            @pl.loop(0, NB)
            def _(b):
                for c in range(3):
                    at = pl.multiple_of(b * 16, 16)
                    stage[c, pl.ds(at, 16), :] = buf[b, :, first + c, :].astype(jnp.bfloat16)


def unpack_cols(buf, stage, sy):
    for side, first, other in ((0, 24, 5), (1, 5, 24)):

        @pl.when(sy == side)
        def _():
            @pl.loop(0, NB)
            def _(b):
                for c in range(3):
                    at = pl.multiple_of(b * 16, 16)
                    buf[b, :, first + c, :] = stage[c, pl.ds(at, 16), :].astype(jnp.float32)
                    buf[b, :, other + c, :] = jnp.zeros((PR, 128), jnp.float32)


def lanes(b):
    return pl.ds(pl.multiple_of(b * 128, 128), 128)


def depthwise(buf, b, taps, start, flip):
    acc = start
    for j in range(KW):
        jj = 6 - j if flip else j
        shifted = buf[b, 0:14, 5 + jj : 21 + jj, :]
        for i in range(KW):
            ii = 6 - i if flip else i
            acc = acc + taps[i, j, lanes(b)].reshape(1, 1, 128) * shifted[ii : ii + ROWS]
    return acc


def kernel_grad(xbuf, gbuf, grads, b):
    g = gbuf[b, 3:11, 8:24, :]
    for j in range(KW):
        shifted = xbuf[b, 0:14, 5 + j : 21 + j, :]
        for i in range(KW):
            q = jnp.sum(g * shifted[i : i + ROWS], axis=0)
            grads[b * 7 + i, j, :] = jnp.sum(q, axis=0)


TOK = ROWS * COLS


def block_kernel(
    code, expo, cot, taps, dw_bias_in, ln_gain_in, ln_bias_in, w_up, b_up, w_down, b_down_in, layer_scale_in,
    bo, gi, gk, gg, gs,
    dw_bias, ln_gain, ln_bias, b_down, layer_scale, xp, gp, stage, landed, up, down, ln, dm, conv, rstd, pre, dact, act, dpre,
    mine_dln, send_dln, got_dln, mine_mlp, send_mlp, got_mlp,
    grads, got1, part, got2, fin, full,
    ls, vs, xus, xur, xds, xdr, a1s, a1r, azs, azr, bzs, bzr, bys, byr, bfs, bfr, ts, tr, dls, dlr, mls, mlr,
    hs, hr, cs, cr, s1, r1, s2, r2, s3, r3, s4, r4,
):
    sx, sy, f = lax.axis_index("sx"), lax.axis_index("sy"), lax.axis_index("fsdp")
    g = sx * 2 + sy
    half = lax.rem(sx, 2)
    other = {"sx": sx + 1 - 2 * half}
    z, y = f // 4, lax.rem(f, 4)
    f32, bf16 = jnp.float32, jnp.bfloat16

    def peer(k):
        p = lax.rem(g + k, 8)
        return p, {"sx": p // 2, "sy": lax.rem(p, 2)}

    x = sy * 2 + sx // 2
    odd_x = lax.rem(x, 2)
    missing = lambda buf: MISSING_UP if buf is up else MISSING_DOWN

    def x_peer(sign):
        to = lax.rem(x + sign + 4, 4)
        return {"sx": lax.rem(to, 2) * 2 + half, "sy": to // 2}

    def zz(d):
        return lax.rem(z + d + 8, 8)

    def yy(d):
        return lax.rem(y + d + 4, 4)

    def window(buf, start=0):
        return pl.ds(pl.multiple_of(start + odd_x * missing(buf), 128), CHANS - missing(buf))

    def shard(buf, dz, dy):
        return buf.at[pl.ds(pl.multiple_of((zz(dz) * 4 + yy(dy)) * 48, 16), 48), window(buf)]

    barrier = pltpu.get_barrier_semaphore()
    near = [{"fsdp": zz(1) * 4 + y}, {"fsdp": zz(-1) * 4 + y}]
    near += [{"fsdp": z * 4 + yy(k)} for k in (1, 2, 3)] + [peer(k)[1] for k in range(1, 8)]
    for where in near:
        pl.semaphore_signal(barrier, inc=1, device_id=where, device_id_type=MESH)

    own = [
        pltpu.make_async_copy(w_up.at[:, window(up, half * HID)], shard(up, 0, 0), ls.at[0]),
        pltpu.make_async_copy(w_down.at[:, window(down, half * HID)], shard(down, 0, 0), ls.at[1]),
    ]
    vectors = (
        (dw_bias_in, dw_bias), (ln_gain_in, ln_gain), (ln_bias_in, ln_bias), (b_down_in, b_down),
        (layer_scale_in, layer_scale),
    )
    rows_in = [pltpu.make_async_copy(src, dst.at[0], vs.at[n]) for n, (src, dst) in enumerate(vectors)]
    for copy in own + rows_in:
        copy.start()
    for copy in own:
        copy.wait()
    pl.semaphore_wait(barrier, len(near))

    sent = []

    def send(copy):
        copy.start()
        sent.append(copy)

    def up_y(k):
        return remote(shard(up, 0, 0), shard(up, 0, 0), a1s.at[k - 1], a1r.at[k - 1], {"fsdp": z * 4 + yy(k)})

    def up_y_got(k):
        return remote(shard(up, 0, -k), shard(up, 0, -k), a1s.at[k - 1], a1r.at[k - 1], {"fsdp": z * 4 + yy(k)})

    def up_z(way, k, s, got=False):
        sign = 1 - 2 * way
        block = shard(up, -sign * (s if got else s - 1), -k)
        at = way * 16 + k * 4 + s - 1
        return remote(block, block, azs.at[at], azr.at[at], {"fsdp": zz(sign) * 4 + y})

    def down_z(way, s, got=False):
        sign = 1 - 2 * way
        block = shard(down, -sign * (s if got else s - 1), 0)
        at = way * 4 + s - 1
        return remote(block, block, bzs.at[at], bzr.at[at], {"fsdp": zz(sign) * 4 + y})

    def down_y(way, d, got=False):
        sign = 1 - 2 * way
        block = shard(down, d, -sign if got else 0)
        at = way * 8 + d
        return remote(block, block, bys.at[at], byr.at[at], {"fsdp": z * 4 + yy(sign)})

    def down_on(d, got=False):
        sign = 1 - 2 * (d % 2)
        block = shard(down, d, 2 if got else -sign)
        return remote(block, block, bfs.at[d], bfr.at[d], {"fsdp": z * 4 + yy(sign)})

    def x_send(buf, d, dy, got=False):
        sends, recvs = (xus, xur) if buf is up else (xds, xdr)
        at = d % 8 * 4 + dy % 4
        rows = pl.ds(pl.multiple_of((zz(d) * 4 + yy(dy)) * 48, 16), 48)
        place = (1 - odd_x if got else odd_x) * (CHANS - missing(buf))
        block = buf.at[rows, pl.ds(pl.multiple_of(place, 128), missing(buf))]
        return remote(block, block, sends.at[at], recvs.at[at], x_peer(1 - 2 * ((d + dy) % 2)))

    def x_arrived(buf, step):
        for d in sorted({-step % 8, step}):
            for dy in (0, 1, -1, 2):
                x_send(buf, d, dy, True).wait_recv()

    def handle(kind, way, k=0, s=0):
        if kind == "uy":
            up_y_got(way).wait_recv()
            for to in (0, 1):
                send(up_z(to, way, 1))
            send(x_send(up, 0, -way))
        elif kind == "uz":
            up_z(way, k, s, True).wait_recv()
            if s < (4 if way == k // 2 else 3):
                send(up_z(way, k, s + 1))
            send(x_send(up, s if way else -s, -k))
        elif kind == "dz":
            down_z(way, k, True).wait_recv()
            if k < 4 - way:
                send(down_z(way, k + 1))
            d = k if way else 8 - k
            send(down_y(0, d))
            send(down_y(1, d))
            send(x_send(down, d, 0))
        elif kind == "dy":
            down_y(way, k, True).wait_recv()
            if k % 2 == way:
                send(down_on(k))
            send(x_send(down, k, 1 if way else -1))
        else:
            down_on(way, True).wait_recv()
            send(x_send(down, way, 2))

    send(up_y(1))
    send(up_y(3))
    for way in (0, 1):
        send(up_z(way, 0, 1))
        send(down_z(way, 1))
    send(up_y(2))
    for way in (0, 1):
        send(down_y(way, 0))
    send(x_send(up, 0, 0))
    send(x_send(down, 0, 0))

    for b in range(NB):
        at = slice(b * 128, (b + 1) * 128)
        factor = jnp.left_shift(1, expo[b] + 2).astype(f32) * 0.25
        scaled = code[:, :, at].astype(f32) * factor[:, :, None]
        xp[b, 3:11, 8:24, :] = scaled
    zero_rows(xp, sx)
    row_halo(xp, hs.at[0], hr.at[0], sx, "start")

    def tokens(buf, at):
        return remote(buf.at[0:TOK], buf.at[TOK : 2 * TOK], ts.at[at], tr.at[at], other)

    def forward_conv(b):
        start = jnp.broadcast_to(dw_bias[:, lanes(b)].reshape(1, 1, 128), (ROWS, COLS, 128))
        conv[b] = depthwise(xp, b, taps, start, False).reshape(TOK, 128)

    xcol = remote(stage.at[0], landed.at[0], cs.at[0], cr.at[0], {"sy": 1 - sy})

    def tokens_task():
        for copy in rows_in:
            copy.wait()

        @pl.loop(0, NB)
        def _(b):
            ct = cot[:, :, lanes(b)].astype(f32).reshape(TOK, 128)
            dm[0:TOK, lanes(b)] = (layer_scale[:, lanes(b)] * ct).astype(bf16)

        send(tokens(dm, 0))
        zero_rows(gp, sx)
        grads[84:88] = jnp.zeros((4, 8, 128), f32)

    def xcols_task():
        row_halo(xp, hs.at[0], hr.at[0], sx, "wait")
        pack_cols(xp, stage.at[0], sy)
        xcol.start()

    def unpack_task():
        xcol.wait()
        unpack_cols(xp, landed.at[0], sy)

    def norm_task():
        def over_channels(term):
            total = lax.fori_loop(0, NB, lambda b, t: t + term(b), jnp.zeros((TOK, 128), f32))
            return jnp.sum(total, axis=1, keepdims=True) / CHANS

        mu = over_channels(lambda b: conv[b])
        var = over_channels(lambda b: (conv[b] - mu) * (conv[b] - mu))
        rstd[...] = jnp.broadcast_to(lax.rsqrt(var + 1e-6), (TOK, 128))

        @pl.loop(0, NB)
        def _(b):
            normed = (conv[b] - mu) * rstd[...]
            conv[b] = normed
            ln[0:TOK, lanes(b)] = (normed * ln_gain[:, lanes(b)] + ln_bias[:, lanes(b)]).astype(bf16)

        send(tokens(ln, 1))

    odd = lax.rem(z, 2)

    def wide(n):
        return pl.ds(pl.multiple_of(n * 512, 512), 512)

    def add_pre(s):
        base = (-odd, -2 + 3 * odd, 2 - 5 * odd, 4 - odd)[s - 1]
        rows = pl.ds(pl.multiple_of(zz(base) * 192, 384), 384)

        @pl.loop(0, 3)
        def _(n):
            term = jnp.dot(ln[:, rows], up[rows, wide(n)], preferred_element_type=f32)
            if s == 1:
                start = pl.multiple_of(half * HID + n * 512, 512)
                pre[:, wide(n)] = term + b_up[:, pl.ds(start, 512)]
            else:
                pre[:, wide(n)] = pre[:, wide(n)] + term

    def add_dact(s):
        base = (-odd, -2 + 3 * odd, 2 - 5 * odd, 4 - odd)[s - 1]
        rows = pl.ds(pl.multiple_of(zz(base) * 192, 384), 384)

        @pl.loop(0, 3)
        def _(n):
            term = jnp.dot(dm[:, rows], down[rows, wide(n)], preferred_element_type=f32)
            dact[:, wide(n)] = term if s == 1 else dact[:, wide(n)] + term

    for name, *rest in ORDER:
        if name == "tokens":
            tokens_task()
        elif name == "xcols":
            xcols_task()
        elif name == "unpack":
            unpack_task()
        elif name == "conv":
            pl.loop(rest[0], rest[0] + 3)(forward_conv)
        elif name == "norm":
            norm_task()
        elif name == "pre":
            if rest[0] == 1:
                tokens(ln, 1).wait_recv()
                x_arrived(up, 0)
            x_arrived(up, rest[0])
            add_pre(rest[0])
        elif name == "back":
            if rest[0] == 1:
                tokens(dm, 0).wait_recv()
                x_arrived(down, 0)
            x_arrived(down, rest[0])
            add_dact(rest[0])
        else:
            handle(name, *rest)

    @pl.loop(0, 12)
    def _(n):
        v = pre[:, lanes(n)]
        v2 = v * v
        t = jnp.tanh(GELU_C * v * (1.0 + 0.044715 * v2))
        cdf = 0.5 * (1.0 + t)
        act[:, lanes(n)] = (v * cdf).astype(bf16)
        slope = cdf + 0.5 * v * (1.0 - t * t) * (GELU_C * (1.0 + 3 * 0.044715 * v2))
        dpre[:, lanes(n)] = (dact[:, lanes(n)] * slope).astype(bf16)

    moved_dln = (send_dln, got_dln, dls, dlr)
    moved_mlp = (send_mlp, got_mlp, mls, mlr)

    def arrived(moved, n):
        src, dst, sends, recvs = moved
        return remote(src.at[:, wide(n)], dst.at[:, wide(n)], sends.at[n], recvs.at[n], other)

    def down_projection(lhs, weights, mine, moved):
        @pl.loop(0, 3)
        def _(n):
            out = lax.dot_general(
                lhs[...], weights[wide(n), :], (((1,), (1,)), ((), ())), preferred_element_type=f32
            )
            mine[:, wide(n)] = out[0:TOK]
            moved[0][:, wide(n)] = out[TOK : 2 * TOK]
            arrived(moved, n).start()

    down_projection(dpre, up, mine_dln, moved_dln)
    down_projection(act, down, mine_mlp, moved_mlp)

    def back_sums(b, sums):
        @pl.when(lax.rem(b, 4) == 0)
        def _():
            arrived(moved_dln, b // 4).wait_recv()

        d_ln = mine_dln[:, lanes(b)] + got_dln[:, lanes(b)]
        grads[b * 7, 7, :] = jnp.sum(d_ln * conv[b], axis=0)
        d_norm = d_ln * ln_gain[:, lanes(b)]
        mine_dln[:, lanes(b)] = d_norm
        return sums[0] + d_norm, sums[1] + d_norm * conv[b]

    zeros = jnp.zeros((TOK, 128), f32)
    sum_d, sum_dn = lax.fori_loop(0, NB, back_sums, (zeros, zeros))
    mean_d = jnp.sum(sum_d, axis=1, keepdims=True) / CHANS
    mean_dn = jnp.sum(sum_dn, axis=1, keepdims=True) / CHANS

    @pl.loop(0, NB)
    def _(b):
        d_conv = rstd[...] * (mine_dln[:, lanes(b)] - mean_d - conv[b] * mean_dn)
        gp[b, 3:11, 8:24, :] = d_conv.reshape(ROWS, COLS, 128)

    row_halo(gp, hs.at[1], hr.at[1], sx, "start")

    @pl.loop(0, 8)
    def _(b):
        kernel_grad(xp, gp, grads, b)

    row_halo(gp, hs.at[1], hr.at[1], sx, "wait")
    pack_cols(gp, stage.at[1], sy)
    col = remote(stage.at[1], landed.at[1], cs.at[1], cr.at[1], {"sy": 1 - sy})
    col.start()

    @pl.loop(0, NB)
    def _(b):
        @pl.when(lax.rem(b, 4) == 0)
        def _():
            arrived(moved_mlp, b // 4).wait_recv()

        mlp = (mine_mlp[:, lanes(b)] + got_mlp[:, lanes(b)]) + b_down[:, lanes(b)]
        ct = cot[:, :, lanes(b)].astype(jnp.float32).reshape(TOK, 128)
        grads[b * 7 + 1, 7, :] = jnp.sum(ct * mlp, axis=0)
        scaled = xp[b, 3:11, 8:24, :].reshape(TOK, 128)
        bo[:, lanes(b)] = (scaled + layer_scale[:, lanes(b)] * mlp).astype(jnp.bfloat16)
        for i in range(2, 7):
            grads[b * 7 + i, 7, :] = jnp.zeros((128,), jnp.float32)

    @pl.loop(8, NB)
    def _(b):
        kernel_grad(xp, gp, grads, b)

    first = []
    for k in range(1, 8):
        p, where = peer(k)
        first.append(remote(grads.at[pl.ds(p * PIECE, PIECE)], got1.at[k - 1], s1.at[k - 1], r1.at[k - 1], where))
        first[-1].start()

    col.wait()
    unpack_cols(gp, landed.at[1], sy)

    def out_conv(b):
        gi[:, :, lanes(b)] = depthwise(
            gp, b, taps, cot[:, :, lanes(b)].astype(jnp.float32), True
        ).astype(jnp.bfloat16)

    pl.loop(0, 4)(out_conv)

    total = grads[pl.ds(g * PIECE, PIECE)]
    for k in range(7):
        first[k].wait_recv()
        total = total + got1[k]
    part[...] = total

    def to_owner(t):
        owner = t * 3
        slot = lax.rem(f - owner + 32, 32)
        return remote(part.at[t], got2.at[slot], s2.at[t], r2.at[slot], {"fsdp": owner})

    for t in range(PIECE):

        @pl.when(f != t * 3)
        def _():
            to_owner(t).start()

    pl.loop(4, 8)(out_conv)

    mine = f // 3
    owns = lax.rem(f, 3) == 0

    def spread(k):
        return remote(fin.at[mine], fin.at[mine], s3.at[k], r3.at[mine], {"fsdp": lax.rem(f + k, 32)})

    @pl.when(owns)
    def _():
        fin[mine] = part[mine]

        @pl.loop(1, 32)
        def _(k):
            remote(part.at[0], got2.at[k], s2.at[0], r2.at[k], {"fsdp": f}).wait_recv()
            fin[mine] = fin[mine] + got2[k]

        @pl.loop(1, 32)
        def _(k):
            spread(k).start()

    pl.loop(8, NB)(out_conv)

    for t in range(PIECE):

        @pl.when(f != t * 3)
        def _():
            remote(fin.at[t], fin.at[t], s3.at[0], r3.at[t], {"fsdp": t * 3}).wait_recv()

    last = []
    for k in range(1, 8):
        p, where = peer(k)
        last.append(remote(fin, full.at[pl.ds(g * PIECE, PIECE)], s4.at[k - 1], r4.at[k - 1], where))
        last[-1].start()
    full[pl.ds(g * PIECE, PIECE)] = fin[...]
    for k in range(7):
        last[k].wait_recv()
    for b in range(NB):
        at = slice(b * 128, (b + 1) * 128)
        for i in range(KW):
            gk[i, :, at] = full[b * 7 + i, 0:7, :]
        gg[at] = full[b * 7, 7, :]
        gs[at] = full[b * 7 + 1, 7, :]

    for k in range(7):
        first[k].wait_send()
        last[k].wait_send()
    for t in range(PIECE):

        @pl.when(f != t * 3)
        def _():
            to_owner(t).wait_send()

    @pl.when(owns)
    def _():
        @pl.loop(1, 32)
        def _(k):
            spread(k).wait_send()

    for n in range(3):
        arrived(moved_dln, n).wait_send()
        arrived(moved_mlp, n).wait_send()
    for copy in sent:
        copy.wait_send()


def on_device(
    x_code, x_exp, dw_kernel, dw_bias, ln_gain, ln_bias, w_up, b_up, w_down, b_down, layer_scale, cotangent
):
    vmem = pl.BlockSpec(memory_space=pltpu.VMEM)
    anywhere = pl.BlockSpec(memory_space=pl.ANY)
    dma = pltpu.SemaphoreType.DMA
    f32, bf16 = jnp.float32, jnp.bfloat16
    row = lambda v: v.reshape(1, -1)
    tok_f32 = pltpu.VMEM((TOK, CHANS), f32)
    pair_f32, pair_bf16 = pltpu.VMEM((2 * TOK, HID), f32), pltpu.VMEM((2 * TOK, HID), bf16)
    weight = pltpu.VMEM((CHANS, HID), bf16)
    padded = pltpu.VMEM((NB, PR, PC, 128), f32)
    staged = pltpu.VMEM((2, 3, NB * 16, 128), bf16)
    block_out, grad_input, grad_kernel, grad_gain, grad_scale = pl.pallas_call(
        block_kernel,
        out_shape=(
            jax.ShapeDtypeStruct((TOK, CHANS), bf16),
            jax.ShapeDtypeStruct((ROWS, COLS, CHANS), bf16),
            jax.ShapeDtypeStruct((KW, KW, CHANS), f32),
            jax.ShapeDtypeStruct((CHANS,), f32),
            jax.ShapeDtypeStruct((CHANS,), f32),
        ),
        in_specs=[vmem] * 4 + [anywhere] * 4 + [vmem] + [anywhere] * 3,
        out_specs=(vmem,) * 5,
        scratch_shapes=[
            *[pltpu.VMEM((1, CHANS), f32)] * 5, padded, padded, staged, staged, weight, weight, pair_bf16, pair_bf16,
            pltpu.VMEM((NB, TOK, 128), f32), pltpu.VMEM((TOK, 128), f32),
            pair_f32, pair_f32, pair_bf16, pair_bf16,
            tok_f32, tok_f32, tok_f32, tok_f32, tok_f32, tok_f32,
            pltpu.VMEM((88, 8, 128), f32),
            pltpu.VMEM((7, PIECE, 8, 128), f32),
            pltpu.VMEM((PIECE, 8, 128), f32),
            pltpu.VMEM((32, 8, 128), f32),
            pltpu.VMEM((PIECE, 8, 128), f32),
            pltpu.VMEM((88, 8, 128), f32),
            dma((2,)), dma((5,)), dma((32,)), dma((32,)), dma((32,)), dma((32,)),
            dma((3,)), dma((3,)), dma((32,)), dma((32,)), dma((8,)), dma((8,)),
            dma((16,)), dma((16,)), dma((8,)), dma((8,)), dma((2,)), dma((2,)),
            dma((6,)), dma((6,)), dma((6,)), dma((6,)),
            dma((2, 2)), dma((2, 2)), dma((2,)), dma((2,)),
            dma((7,)), dma((7,)), dma((PIECE,)), dma((32,)),
            dma((32,)), dma((PIECE,)), dma((7,)), dma((7,)),
        ],
        compiler_params=pltpu.CompilerParams(
            collective_id=1, has_side_effects=True, vmem_limit_bytes=56 * 2**20
        ),
        name="block",
    )(
        x_code[0], x_exp[0].transpose(2, 0, 1), cotangent[0], dw_kernel, dw_bias, ln_gain, ln_bias,
        w_up, row(b_up), w_down.T, b_down, layer_scale,
    )
    return (
        block_out.reshape(1, ROWS, COLS, CHANS), grad_input[None], grad_kernel, grad_gain, grad_scale
    )


def solution(mesh):
    placed = (
        P("fsdp", "sx", "sy", None),
        P("fsdp", "sx", "sy", None),
        P(),
        P(),
        P(),
        P(),
        P("fsdp", None),
        P(),
        P(None, "fsdp"),
        P(),
        P(),
        P("fsdp", "sx", "sy", None),
    )
    return jax.shard_map(
        on_device,
        mesh=mesh,
        in_specs=placed,
        out_specs=(P("fsdp", "sx", "sy", None), P("fsdp", "sx", "sy", None), P(), P(), P()),
        check_vma=False,
    )
```

```python
import jax
import jax.numpy as jnp
from jax import lax
from jax.experimental import pallas as pl
from jax.experimental.pallas import tpu as pltpu
from jax.sharding import PartitionSpec as P

CG = 128
KW = 7
NB = 12
ROWS, COLS, CHANS = 8, 16, 1536
PR, PC = 16, 32
PIECE = 11
HID = 1536
MISSING_UP, MISSING_DOWN = 640, 512
ORDER = (
    ("uz", 0, 0, 1), ("uz", 1, 0, 1), ("uy", 1), ("uy", 3), ("uy", 2), ("tokens",), ("dz", 0, 1),
    ("dz", 1, 1), ("dy", 0, 0), ("dy", 1, 0), ("xcols",), ("uz", 0, 0, 2), ("uz", 1, 0, 2), ("dy", 0, 7),
    ("dy", 1, 7), ("uz", 0, 1, 1), ("uz", 1, 1, 1), ("uz", 0, 3, 1), ("uz", 1, 3, 1), ("dy", 0, 1),
    ("dy", 1, 1), ("do", 0), ("dz", 0, 2), ("dz", 1, 2), ("uz", 0, 2, 1), ("uz", 1, 2, 1), ("unpack",),
    ("conv", 0), ("do", 7), ("dy", 0, 6), ("uz", 0, 0, 3), ("uz", 1, 0, 3), ("conv", 3), ("do", 1),
    ("dy", 1, 6), ("dy", 0, 2), ("uz", 0, 1, 2), ("uz", 1, 1, 2), ("conv", 6), ("dz", 0, 3), ("dz", 1, 3),
    ("dy", 1, 2), ("uz", 0, 3, 2), ("uz", 1, 3, 2), ("conv", 9), ("do", 6), ("norm",), ("dy", 1, 5),
    ("uz", 0, 2, 2), ("uz", 1, 2, 2), ("do", 2), ("dy", 0, 5), ("dy", 1, 3), ("uz", 0, 0, 4),
    ("uz", 1, 1, 3), ("back", 1), ("dz", 0, 4), ("dy", 0, 3), ("uz", 0, 1, 3), ("uz", 1, 3, 3), ("pre", 1),
    ("uz", 1, 2, 3), ("do", 5), ("dy", 0, 4), ("back", 2), ("uz", 0, 3, 3), ("do", 3), ("dy", 1, 4),
    ("uz", 1, 3, 4), ("uz", 0, 2, 3), ("pre", 2), ("uz", 1, 2, 4), ("uz", 0, 1, 4), ("do", 4), ("back", 3),
    ("pre", 3), ("pre", 4), ("back", 4),
)
GELU_C = 0.7978845608028654
MESH = pl.DeviceIdType.MESH


def remote(src, dst, send, recv, where):
    return pltpu.make_async_remote_copy(
        src_ref=src, dst_ref=dst, send_sem=send, recv_sem=recv, device_id=where, device_id_type=MESH
    )


def row_halo(buf, send, recv, sx, act):
    down = remote(buf.at[:, 8:11, 8:24, :], buf.at[:, 0:3, 8:24, :], send.at[0], recv.at[0], {"sx": sx + 1})
    up = remote(buf.at[:, 3:6, 8:24, :], buf.at[:, 11:14, 8:24, :], send.at[1], recv.at[1], {"sx": sx - 1})
    if act == "start":

        @pl.when(sx < 3)
        def _():
            down.start()

        @pl.when(sx > 0)
        def _():
            up.start()

    else:

        @pl.when(sx < 3)
        def _():
            up.wait_recv()
            down.wait_send()

        @pl.when(sx > 0)
        def _():
            down.wait_recv()
            up.wait_send()


def zero_rows(buf, sx):
    @pl.when(sx == 0)
    def _():
        buf[:, 0:3, :, :] = jnp.zeros((NB, 3, PC, 128), jnp.float32)

    @pl.when(sx == 3)
    def _():
        buf[:, 11:14, :, :] = jnp.zeros((NB, 3, PC, 128), jnp.float32)


def pack_cols(buf, stage, sy):
    for side, first in ((0, 21), (1, 8)):

        @pl.when(sy == side)
        def _():
            @pl.loop(0, NB)
            def _(b):
                for c in range(3):
                    at = pl.multiple_of(b * 16, 16)
                    stage[c, pl.ds(at, 16), :] = buf[b, :, first + c, :].astype(jnp.bfloat16)


def unpack_cols(buf, stage, sy):
    for side, first, other in ((0, 24, 5), (1, 5, 24)):

        @pl.when(sy == side)
        def _():
            @pl.loop(0, NB)
            def _(b):
                for c in range(3):
                    at = pl.multiple_of(b * 16, 16)
                    buf[b, :, first + c, :] = stage[c, pl.ds(at, 16), :].astype(jnp.float32)
                    buf[b, :, other + c, :] = jnp.zeros((PR, 128), jnp.float32)


def lanes(b):
    return pl.ds(pl.multiple_of(b * 128, 128), 128)


def depthwise(buf, b, taps, start, flip):
    acc = start
    for j in range(KW):
        jj = 6 - j if flip else j
        shifted = buf[b, 0:14, 5 + jj : 21 + jj, :]
        for i in range(KW):
            ii = 6 - i if flip else i
            acc = acc + taps[i, j, lanes(b)].reshape(1, 1, 128) * shifted[ii : ii + ROWS]
    return acc


def kernel_grad(xbuf, gbuf, grads, b):
    g = gbuf[b, 3:11, 8:24, :]
    for j in range(KW):
        shifted = xbuf[b, 0:14, 5 + j : 21 + j, :]
        for i in range(KW):
            q = jnp.sum(g * shifted[i : i + ROWS], axis=0)
            grads[b * 7 + i, j, :] = jnp.sum(q, axis=0)


TOK = ROWS * COLS


def block_kernel(
    code, expo, cot, taps, dw_bias_in, ln_gain_in, ln_bias_in, w_up, b_up, w_down, b_down_in, layer_scale_in,
    bo, gi, gk, gg, gs,
    dw_bias, ln_gain, ln_bias, b_down, layer_scale, xp, gp, stage, landed, up, down, ln, dm, conv, rstd, pre, dact, act, dpre,
    mine_dln, send_dln, got_dln, mine_mlp, send_mlp, got_mlp,
    grads, got1, part, got2, fin, full,
    ls, vs, xus, xur, xds, xdr, a1s, a1r, azs, azr, bzs, bzr, bys, byr, bfs, bfr, ts, tr, dls, dlr, mls, mlr,
    hs, hr, cs, cr, s1, r1, s2, r2, s3, r3, s4, r4,
):
    sx, sy, f = lax.axis_index("sx"), lax.axis_index("sy"), lax.axis_index("fsdp")
    g = sx * 2 + sy
    half = lax.rem(sx, 2)
    other = {"sx": sx + 1 - 2 * half}
    z, y = f // 4, lax.rem(f, 4)
    f32, bf16 = jnp.float32, jnp.bfloat16

    def peer(k):
        p = lax.rem(g + k, 8)
        return p, {"sx": p // 2, "sy": lax.rem(p, 2)}

    x = sy * 2 + sx // 2
    odd_x = lax.rem(x, 2)
    missing = lambda buf: MISSING_UP if buf is up else MISSING_DOWN

    def x_peer(sign):
        to = lax.rem(x + sign + 4, 4)
        return {"sx": lax.rem(to, 2) * 2 + half, "sy": to // 2}

    def zz(d):
        return lax.rem(z + d + 8, 8)

    def yy(d):
        return lax.rem(y + d + 4, 4)

    def window(buf, start=0):
        return pl.ds(pl.multiple_of(start + odd_x * missing(buf), 128), CHANS - missing(buf))

    def shard(buf, dz, dy):
        return buf.at[pl.ds(pl.multiple_of((zz(dz) * 4 + yy(dy)) * 48, 16), 48), window(buf)]

    barrier = pltpu.get_barrier_semaphore()
    near = [{"fsdp": zz(1) * 4 + y}, {"fsdp": zz(-1) * 4 + y}]
    near += [{"fsdp": z * 4 + yy(k)} for k in (1, 2, 3)] + [peer(k)[1] for k in range(1, 8)]
    for where in near:
        pl.semaphore_signal(barrier, inc=1, device_id=where, device_id_type=MESH)

    own = [
        pltpu.make_async_copy(w_up.at[:, window(up, half * HID)], shard(up, 0, 0), ls.at[0]),
        pltpu.make_async_copy(w_down.at[:, window(down, half * HID)], shard(down, 0, 0), ls.at[1]),
    ]
    vectors = (
        (dw_bias_in, dw_bias), (ln_gain_in, ln_gain), (ln_bias_in, ln_bias), (b_down_in, b_down),
        (layer_scale_in, layer_scale),
    )
    rows_in = [pltpu.make_async_copy(src, dst.at[0], vs.at[n]) for n, (src, dst) in enumerate(vectors)]
    for copy in own + rows_in:
        copy.start()
    for copy in own:
        copy.wait()
    pl.semaphore_wait(barrier, len(near))

    sent = []

    def send(copy):
        copy.start()
        sent.append(copy)

    def up_y(k):
        return remote(shard(up, 0, 0), shard(up, 0, 0), a1s.at[k - 1], a1r.at[k - 1], {"fsdp": z * 4 + yy(k)})

    def up_y_got(k):
        return remote(shard(up, 0, -k), shard(up, 0, -k), a1s.at[k - 1], a1r.at[k - 1], {"fsdp": z * 4 + yy(k)})

    def up_z(way, k, s, got=False):
        sign = 1 - 2 * way
        block = shard(up, -sign * (s if got else s - 1), -k)
        at = way * 16 + k * 4 + s - 1
        return remote(block, block, azs.at[at], azr.at[at], {"fsdp": zz(sign) * 4 + y})

    def down_z(way, s, got=False):
        sign = 1 - 2 * way
        block = shard(down, -sign * (s if got else s - 1), 0)
        at = way * 4 + s - 1
        return remote(block, block, bzs.at[at], bzr.at[at], {"fsdp": zz(sign) * 4 + y})

    def down_y(way, d, got=False):
        sign = 1 - 2 * way
        block = shard(down, d, -sign if got else 0)
        at = way * 8 + d
        return remote(block, block, bys.at[at], byr.at[at], {"fsdp": z * 4 + yy(sign)})

    def down_on(d, got=False):
        sign = 1 - 2 * (d % 2)
        block = shard(down, d, 2 if got else -sign)
        return remote(block, block, bfs.at[d], bfr.at[d], {"fsdp": z * 4 + yy(sign)})

    def x_send(buf, d, dy, got=False):
        sends, recvs = (xus, xur) if buf is up else (xds, xdr)
        at = d % 8 * 4 + dy % 4
        rows = pl.ds(pl.multiple_of((zz(d) * 4 + yy(dy)) * 48, 16), 48)
        place = (1 - odd_x if got else odd_x) * (CHANS - missing(buf))
        block = buf.at[rows, pl.ds(pl.multiple_of(place, 128), missing(buf))]
        return remote(block, block, sends.at[at], recvs.at[at], x_peer(1 - 2 * ((d + dy) % 2)))

    def x_arrived(buf, step):
        for d in sorted({-step % 8, step}):
            for dy in (0, 1, -1, 2):
                x_send(buf, d, dy, True).wait_recv()

    def handle(kind, way, k=0, s=0):
        if kind == "uy":
            up_y_got(way).wait_recv()
            for to in (0, 1):
                send(up_z(to, way, 1))
            send(x_send(up, 0, -way))
        elif kind == "uz":
            up_z(way, k, s, True).wait_recv()
            if s < (4 if way == k // 2 else 3):
                send(up_z(way, k, s + 1))
            send(x_send(up, s if way else -s, -k))
        elif kind == "dz":
            down_z(way, k, True).wait_recv()
            if k < 4 - way:
                send(down_z(way, k + 1))
            d = k if way else 8 - k
            send(down_y(0, d))
            send(down_y(1, d))
            send(x_send(down, d, 0))
        elif kind == "dy":
            down_y(way, k, True).wait_recv()
            if k % 2 == way:
                send(down_on(k))
            send(x_send(down, k, 1 if way else -1))
        else:
            down_on(way, True).wait_recv()
            send(x_send(down, way, 2))

    send(up_y(1))
    send(up_y(3))
    for way in (0, 1):
        send(up_z(way, 0, 1))
        send(down_z(way, 1))
    send(up_y(2))
    for way in (0, 1):
        send(down_y(way, 0))
    send(x_send(up, 0, 0))
    send(x_send(down, 0, 0))

    for b in range(NB):
        at = slice(b * 128, (b + 1) * 128)
        factor = jnp.left_shift(1, expo[b] + 2).astype(f32) * 0.25
        scaled = code[:, :, at].astype(f32) * factor[:, :, None]
        xp[b, 3:11, 8:24, :] = scaled
    zero_rows(xp, sx)
    row_halo(xp, hs.at[0], hr.at[0], sx, "start")

    def tokens(buf, at):
        return remote(buf.at[0:TOK], buf.at[TOK : 2 * TOK], ts.at[at], tr.at[at], other)

    def forward_conv(b):
        start = jnp.broadcast_to(dw_bias[:, lanes(b)].reshape(1, 1, 128), (ROWS, COLS, 128))
        conv[b] = depthwise(xp, b, taps, start, False).reshape(TOK, 128)

    xcol = remote(stage.at[0], landed.at[0], cs.at[0], cr.at[0], {"sy": 1 - sy})

    def tokens_task():
        for copy in rows_in:
            copy.wait()

        @pl.loop(0, NB)
        def _(b):
            ct = cot[:, :, lanes(b)].astype(f32).reshape(TOK, 128)
            dm[0:TOK, lanes(b)] = (layer_scale[:, lanes(b)] * ct).astype(bf16)

        send(tokens(dm, 0))
        zero_rows(gp, sx)
        grads[84:88] = jnp.zeros((4, 8, 128), f32)

    def xcols_task():
        row_halo(xp, hs.at[0], hr.at[0], sx, "wait")
        pack_cols(xp, stage.at[0], sy)
        xcol.start()

    def unpack_task():
        xcol.wait()
        unpack_cols(xp, landed.at[0], sy)

    def norm_task():
        def over_channels(term):
            total = lax.fori_loop(0, NB, lambda b, t: t + term(b), jnp.zeros((TOK, 128), f32))
            return jnp.sum(total, axis=1, keepdims=True) / CHANS

        mu = over_channels(lambda b: conv[b])
        var = over_channels(lambda b: (conv[b] - mu) * (conv[b] - mu))
        rstd[...] = jnp.broadcast_to(lax.rsqrt(var + 1e-6), (TOK, 128))

        @pl.loop(0, NB)
        def _(b):
            normed = (conv[b] - mu) * rstd[...]
            conv[b] = normed
            ln[0:TOK, lanes(b)] = (normed * ln_gain[:, lanes(b)] + ln_bias[:, lanes(b)]).astype(bf16)

        send(tokens(ln, 1))

    odd = lax.rem(z, 2)

    def wide(n):
        return pl.ds(pl.multiple_of(n * 512, 512), 512)

    def broad(n):
        return pl.ds(pl.multiple_of(n * 768, 256), 768)

    def add_pre(s):
        base = (-odd, -2 + 3 * odd, 2 - 5 * odd, 4 - odd)[s - 1]
        rows = pl.ds(pl.multiple_of(zz(base) * 192, 384), 384)

        @pl.loop(0, 2)
        def _(n):
            term = jnp.dot(ln[:, rows], up[rows, broad(n)], preferred_element_type=f32)
            if s == 1:
                start = pl.multiple_of(half * HID + n * 768, 256)
                pre[:, broad(n)] = term + b_up[:, pl.ds(start, 768)]
            else:
                pre[:, broad(n)] = pre[:, broad(n)] + term

    def add_dact(s):
        base = (-odd, -2 + 3 * odd, 2 - 5 * odd, 4 - odd)[s - 1]
        rows = pl.ds(pl.multiple_of(zz(base) * 192, 384), 384)

        @pl.loop(0, 2)
        def _(n):
            term = jnp.dot(dm[:, rows], down[rows, broad(n)], preferred_element_type=f32)
            dact[:, broad(n)] = term if s == 1 else dact[:, broad(n)] + term

    for name, *rest in ORDER:
        if name == "tokens":
            tokens_task()
        elif name == "xcols":
            xcols_task()
        elif name == "unpack":
            unpack_task()
        elif name == "conv":
            pl.loop(rest[0], rest[0] + 3)(forward_conv)
        elif name == "norm":
            norm_task()
        elif name == "pre":
            if rest[0] == 1:
                tokens(ln, 1).wait_recv()
                x_arrived(up, 0)
            x_arrived(up, rest[0])
            add_pre(rest[0])
        elif name == "back":
            if rest[0] == 1:
                tokens(dm, 0).wait_recv()
                x_arrived(down, 0)
            x_arrived(down, rest[0])
            add_dact(rest[0])
        else:
            handle(name, *rest)

    @pl.loop(0, 12)
    def _(n):
        v = pre[:, lanes(n)]
        v2 = v * v
        t = jnp.tanh(GELU_C * v * (1.0 + 0.044715 * v2))
        cdf = 0.5 * (1.0 + t)
        act[:, lanes(n)] = (v * cdf).astype(bf16)
        slope = cdf + 0.5 * v * (1.0 - t * t) * (GELU_C * (1.0 + 3 * 0.044715 * v2))
        dpre[:, lanes(n)] = (dact[:, lanes(n)] * slope).astype(bf16)

    moved_dln = (send_dln, got_dln, dls, dlr)
    moved_mlp = (send_mlp, got_mlp, mls, mlr)

    def arrived(moved, n):
        src, dst, sends, recvs = moved
        return remote(src.at[:, wide(n)], dst.at[:, wide(n)], sends.at[n], recvs.at[n], other)

    def down_projection(lhs, weights, mine, moved):
        @pl.loop(0, 3)
        def _(n):
            out = lax.dot_general(
                lhs[...], weights[wide(n), :], (((1,), (1,)), ((), ())), preferred_element_type=f32
            )
            mine[:, wide(n)] = out[0:TOK]
            moved[0][:, wide(n)] = out[TOK : 2 * TOK]
            arrived(moved, n).start()

    down_projection(dpre, up, mine_dln, moved_dln)
    down_projection(act, down, mine_mlp, moved_mlp)

    def back_sums(b, sums):
        @pl.when(lax.rem(b, 4) == 0)
        def _():
            arrived(moved_dln, b // 4).wait_recv()

        d_ln = mine_dln[:, lanes(b)] + got_dln[:, lanes(b)]
        grads[b * 7, 7, :] = jnp.sum(d_ln * conv[b], axis=0)
        d_norm = d_ln * ln_gain[:, lanes(b)]
        mine_dln[:, lanes(b)] = d_norm
        return sums[0] + d_norm, sums[1] + d_norm * conv[b]

    zeros = jnp.zeros((TOK, 128), f32)
    sum_d, sum_dn = lax.fori_loop(0, NB, back_sums, (zeros, zeros))
    mean_d = jnp.sum(sum_d, axis=1, keepdims=True) / CHANS
    mean_dn = jnp.sum(sum_dn, axis=1, keepdims=True) / CHANS

    @pl.loop(0, NB)
    def _(b):
        d_conv = rstd[...] * (mine_dln[:, lanes(b)] - mean_d - conv[b] * mean_dn)
        gp[b, 3:11, 8:24, :] = d_conv.reshape(ROWS, COLS, 128)

    row_halo(gp, hs.at[1], hr.at[1], sx, "start")

    @pl.loop(0, 8)
    def _(b):
        kernel_grad(xp, gp, grads, b)

    row_halo(gp, hs.at[1], hr.at[1], sx, "wait")
    pack_cols(gp, stage.at[1], sy)
    col = remote(stage.at[1], landed.at[1], cs.at[1], cr.at[1], {"sy": 1 - sy})
    col.start()

    @pl.loop(0, NB)
    def _(b):
        @pl.when(lax.rem(b, 4) == 0)
        def _():
            arrived(moved_mlp, b // 4).wait_recv()

        mlp = (mine_mlp[:, lanes(b)] + got_mlp[:, lanes(b)]) + b_down[:, lanes(b)]
        ct = cot[:, :, lanes(b)].astype(jnp.float32).reshape(TOK, 128)
        grads[b * 7 + 1, 7, :] = jnp.sum(ct * mlp, axis=0)
        scaled = xp[b, 3:11, 8:24, :].reshape(TOK, 128)
        bo[:, lanes(b)] = (scaled + layer_scale[:, lanes(b)] * mlp).astype(jnp.bfloat16)
        for i in range(2, 7):
            grads[b * 7 + i, 7, :] = jnp.zeros((128,), jnp.float32)

    @pl.loop(8, NB)
    def _(b):
        kernel_grad(xp, gp, grads, b)

    first = []
    for k in range(1, 8):
        p, where = peer(k)
        first.append(remote(grads.at[pl.ds(p * PIECE, PIECE)], got1.at[k - 1], s1.at[k - 1], r1.at[k - 1], where))
        first[-1].start()

    col.wait()
    unpack_cols(gp, landed.at[1], sy)

    def out_conv(b):
        gi[:, :, lanes(b)] = depthwise(
            gp, b, taps, cot[:, :, lanes(b)].astype(jnp.float32), True
        ).astype(jnp.bfloat16)

    pl.loop(0, 4)(out_conv)

    total = grads[pl.ds(g * PIECE, PIECE)]
    for k in range(7):
        first[k].wait_recv()
        total = total + got1[k]
    part[...] = total

    def to_owner(t):
        owner = t * 3
        slot = lax.rem(f - owner + 32, 32)
        return remote(part.at[t], got2.at[slot], s2.at[t], r2.at[slot], {"fsdp": owner})

    for t in range(PIECE):

        @pl.when(f != t * 3)
        def _():
            to_owner(t).start()

    pl.loop(4, 8)(out_conv)

    mine = f // 3
    owns = lax.rem(f, 3) == 0

    def spread(k):
        return remote(fin.at[mine], fin.at[mine], s3.at[k], r3.at[mine], {"fsdp": lax.rem(f + k, 32)})

    @pl.when(owns)
    def _():
        fin[mine] = part[mine]

        @pl.loop(1, 32)
        def _(k):
            remote(part.at[0], got2.at[k], s2.at[0], r2.at[k], {"fsdp": f}).wait_recv()
            fin[mine] = fin[mine] + got2[k]

        @pl.loop(1, 32)
        def _(k):
            spread(k).start()

    pl.loop(8, NB)(out_conv)

    for t in range(PIECE):

        @pl.when(f != t * 3)
        def _():
            remote(fin.at[t], fin.at[t], s3.at[0], r3.at[t], {"fsdp": t * 3}).wait_recv()

    last = []
    for k in range(1, 8):
        p, where = peer(k)
        last.append(remote(fin, full.at[pl.ds(g * PIECE, PIECE)], s4.at[k - 1], r4.at[k - 1], where))
        last[-1].start()
    full[pl.ds(g * PIECE, PIECE)] = fin[...]
    for k in range(7):
        last[k].wait_recv()
    for b in range(NB):
        at = slice(b * 128, (b + 1) * 128)
        for i in range(KW):
            gk[i, :, at] = full[b * 7 + i, 0:7, :]
        gg[at] = full[b * 7, 7, :]
        gs[at] = full[b * 7 + 1, 7, :]

    for k in range(7):
        first[k].wait_send()
        last[k].wait_send()
    for t in range(PIECE):

        @pl.when(f != t * 3)
        def _():
            to_owner(t).wait_send()

    @pl.when(owns)
    def _():
        @pl.loop(1, 32)
        def _(k):
            spread(k).wait_send()

    for n in range(3):
        arrived(moved_dln, n).wait_send()
        arrived(moved_mlp, n).wait_send()
    for copy in sent:
        copy.wait_send()


def on_device(
    x_code, x_exp, dw_kernel, dw_bias, ln_gain, ln_bias, w_up, b_up, w_down, b_down, layer_scale, cotangent
):
    vmem = pl.BlockSpec(memory_space=pltpu.VMEM)
    anywhere = pl.BlockSpec(memory_space=pl.ANY)
    dma = pltpu.SemaphoreType.DMA
    f32, bf16 = jnp.float32, jnp.bfloat16
    row = lambda v: v.reshape(1, -1)
    tok_f32 = pltpu.VMEM((TOK, CHANS), f32)
    pair_f32, pair_bf16 = pltpu.VMEM((2 * TOK, HID), f32), pltpu.VMEM((2 * TOK, HID), bf16)
    weight = pltpu.VMEM((CHANS, HID), bf16)
    padded = pltpu.VMEM((NB, PR, PC, 128), f32)
    staged = pltpu.VMEM((2, 3, NB * 16, 128), bf16)
    block_out, grad_input, grad_kernel, grad_gain, grad_scale = pl.pallas_call(
        block_kernel,
        out_shape=(
            jax.ShapeDtypeStruct((TOK, CHANS), bf16),
            jax.ShapeDtypeStruct((ROWS, COLS, CHANS), bf16),
            jax.ShapeDtypeStruct((KW, KW, CHANS), f32),
            jax.ShapeDtypeStruct((CHANS,), f32),
            jax.ShapeDtypeStruct((CHANS,), f32),
        ),
        in_specs=[vmem] * 4 + [anywhere] * 4 + [vmem] + [anywhere] * 3,
        out_specs=(vmem,) * 5,
        scratch_shapes=[
            *[pltpu.VMEM((1, CHANS), f32)] * 5, padded, padded, staged, staged, weight, weight, pair_bf16, pair_bf16,
            pltpu.VMEM((NB, TOK, 128), f32), pltpu.VMEM((TOK, 128), f32),
            pair_f32, pair_f32, pair_bf16, pair_bf16,
            tok_f32, tok_f32, tok_f32, tok_f32, tok_f32, tok_f32,
            pltpu.VMEM((88, 8, 128), f32),
            pltpu.VMEM((7, PIECE, 8, 128), f32),
            pltpu.VMEM((PIECE, 8, 128), f32),
            pltpu.VMEM((32, 8, 128), f32),
            pltpu.VMEM((PIECE, 8, 128), f32),
            pltpu.VMEM((88, 8, 128), f32),
            dma((2,)), dma((5,)), dma((32,)), dma((32,)), dma((32,)), dma((32,)),
            dma((3,)), dma((3,)), dma((32,)), dma((32,)), dma((8,)), dma((8,)),
            dma((16,)), dma((16,)), dma((8,)), dma((8,)), dma((2,)), dma((2,)),
            dma((6,)), dma((6,)), dma((6,)), dma((6,)),
            dma((2, 2)), dma((2, 2)), dma((2,)), dma((2,)),
            dma((7,)), dma((7,)), dma((PIECE,)), dma((32,)),
            dma((32,)), dma((PIECE,)), dma((7,)), dma((7,)),
        ],
        compiler_params=pltpu.CompilerParams(
            collective_id=1, has_side_effects=True, vmem_limit_bytes=56 * 2**20
        ),
        name="block",
    )(
        x_code[0], x_exp[0].transpose(2, 0, 1), cotangent[0], dw_kernel, dw_bias, ln_gain, ln_bias,
        w_up, row(b_up), w_down.T, b_down, layer_scale,
    )
    return (
        block_out.reshape(1, ROWS, COLS, CHANS), grad_input[None], grad_kernel, grad_gain, grad_scale
    )


def solution(mesh):
    placed = (
        P("fsdp", "sx", "sy", None),
        P("fsdp", "sx", "sy", None),
        P(),
        P(),
        P(),
        P(),
        P("fsdp", None),
        P(),
        P(None, "fsdp"),
        P(),
        P(),
        P("fsdp", "sx", "sy", None),
    )
    return jax.shard_map(
        on_device,
        mesh=mesh,
        in_specs=placed,
        out_specs=(P("fsdp", "sx", "sy", None), P("fsdp", "sx", "sy", None), P(), P(), P()),
        check_vma=False,
    )
```
